128 devices in a mesh: row: 8 (over y_lo, x), col: 16 (over y_hi, z, core).
Axes of the slice: x: 4, y: 4 (y_hi: 2, y_lo: 2; y = y_hi * 2 + y_lo), z: 4, core: 2. Of those that a mesh axis runs over, the one named last changes fastest.
Arguments:
- photo_vectors: float32 [16384, 1152], P(('row', 'col')), may hold values from -60 to 60
- sentence_vectors: float32 [16384, 1152], P(('row', 'col')), may hold values from -60 to 60
- matching_index: int32 [16384], replicated, may hold values from 0 to 16383, each once
- natural_warmth_exponent: float32 [1], replicated, may hold values from 4 to 4.8
- shift_term: float32 [1], replicated, may hold values from -4 to -1
Outputs:
- image_grad: float32 [16384, 1152], P(('row', 'col'))
- text_grad: float32 [16384, 1152], P(('row', 'col'))
The draws below stay inside these ranges and needn't reach their ends.
Inputs may be any that keep to these rules, and one draw needn't show every extreme that they name: `matching_index`: every text index appears exactly once.
All inputs are finite; a program needn't handle non-finite values.
Results may differ from the reference program's by a relative error of at most 0.0003.
Values sent between devices are 32-bit elements; how exact they have to be, the bound alone decides.
No kernel may reach another device: no remote copies, remote signals or barrier semaphores. Data moves between devices by JAX's collectives and lax.ppermute only.
A program may use at most 64 MiB of HBM per device.

```python
import math
import jax
import jax.numpy as jnp
from jax import lax

D = 1152
PAIRS = 16384
N_ROW = 8


def row_scales(key, top_scale):
    return jnp.exp(jax.random.uniform(key, (PAIRS, 1), jnp.float32, 0.0, math.log(top_scale)))


def raw_rows(key):
    first, second = jax.random.split(key)
    entries = jnp.clip(jax.random.normal(first, (PAIRS, D), jnp.float32), -6.0, 6.0)
    top_scale = 10.0
    return entries * row_scales(second, top_scale)


def draw_photo_vectors(key, part):
    key = jax.random.fold_in(key, 1)
    return raw_rows(key)


def draw_sentence_vectors(key, part):
    key = jax.random.fold_in(key, 2)
    return raw_rows(key)


def setup_inputs(seed: int = 0) -> dict:
    key_of = jax.random.split(jax.random.key(seed), 6)
    return {
        "photo_vectors": draw_photo_vectors(jax.random.fold_in(key_of[5], 71), 0),
        "sentence_vectors": draw_sentence_vectors(jax.random.fold_in(key_of[5], 71), 0),
        "matching_index": jax.random.permutation(key_of[2], PAIRS).astype(jnp.int32),
        "natural_warmth_exponent": jnp.clip(jax.random.uniform(key_of[3], (1,), jnp.float32, 4.0, 4.8), 4.0, 4.8),
        "shift_term": jnp.clip(jax.random.uniform(key_of[4], (1,), jnp.float32, -4.0, -1.0), -4.0, -1.0),
    }


epsilon = 1e-06

def normalize(raw):
    squares = lax.optimization_barrier(jnp.sum(raw * raw, axis=-1, keepdims=True))
    length = jnp.sqrt(squares + epsilon)
    return (raw / length, length)

def restore_grad(d_unit, unit_vec, length):
    along = lax.optimization_barrier(jnp.sum(unit_vec * d_unit, axis=-1, keepdims=True))
    return (d_unit - unit_vec * along) / length

def reference(photo_vectors, sentence_vectors, matching_index, natural_warmth_exponent, shift_term):
    warmth_multiplier = jnp.exp(natural_warmth_exponent[0])
    tile_start_index = shift_term[0]
    img_unit, img_len = normalize(photo_vectors)
    sentence_normed, txt_len = normalize(sentence_vectors)
    pair_count = photo_vectors.shape[0]
    feat_count = photo_vectors.shape[1]
    block_rows = pair_count // N_ROW
    vertical_values = jnp.arange(pair_count, dtype=jnp.int32)

    def step_block(sentence_derivative, index):
        start = (index * block_rows).astype(jnp.int32)
        photo_tile = lax.dynamic_slice_in_dim(img_unit, start, block_rows, 0)
        matching_indices = lax.dynamic_slice_in_dim(matching_index, start, block_rows, 0)
        similarity_matrix = warmth_multiplier * lax.dot_general(photo_tile, sentence_normed, (((1,), (1,)), ((), ())), precision=lax.Precision.HIGHEST, preferred_element_type=jnp.float32) + tile_start_index
        labels = jnp.where(matching_indices[:, None] == vertical_values[None, :], jnp.float32(1.0), jnp.float32(-1.0))
        similarity_derivative = -labels * jax.nn.sigmoid(-labels * similarity_matrix)
        photo_derivative = warmth_multiplier * jnp.dot(similarity_derivative, sentence_normed, precision=lax.Precision.HIGHEST, preferred_element_type=jnp.float32)
        sentence_derivative = sentence_derivative + warmth_multiplier * lax.dot_general(similarity_derivative, photo_tile, (((0,), (0,)), ((), ())), precision=lax.Precision.HIGHEST, preferred_element_type=jnp.float32)
        return (sentence_derivative, photo_derivative)
    sentence_derivative, d_img_blocks = lax.scan(step_block, jnp.zeros((pair_count, feat_count), jnp.float32), jnp.arange(N_ROW, dtype=jnp.int32))
    photo_derivative = d_img_blocks.reshape(pair_count, feat_count)
    return (restore_grad(photo_derivative, img_unit, img_len), restore_grad(sentence_derivative, sentence_normed, txt_len))
```

```python
import functools

import jax
import jax.numpy as jnp
from jax import lax
from jax.experimental import pallas as pl
from jax.experimental.pallas import tpu as pltpu
from jax.sharding import Mesh
from jax.sharding import PartitionSpec as P

EPS = 1e-06
F32 = jnp.float32
BF16 = jnp.bfloat16
AXES = ("yl", "x", "yh", "z", "c")
PLACES = ((0, 0), (0, 1), (-1, 0), (1, 0), (-1, 1), (1, 1), (2, 0), (2, 1))


def shift_by(value, axis, steps):
    count = lax.axis_size(axis)
    return lax.ppermute(value, axis, [(i, (i + steps) % count) for i in range(count)])


def mm(a, b, ca, cb):
    return lax.dot_general(a, b, (((ca,), (cb,)), ((), ())), preferred_element_type=F32)


def halves(x):
    hi = x.astype(BF16)
    return hi, (x - hi.astype(F32)).astype(BF16)


def normalize_kernel(warmth, photo, text, photo_scaled, photo_unit, photo_len, text_unit, text_len):
    for raw, unit, length in ((photo, photo_unit, photo_len), (text, text_unit, text_len)):
        x = raw[...]
        size = jnp.sqrt(jnp.sum(x * x, axis=-1, keepdims=True) + EPS)
        unit[...] = x / size
        length[...] = size
    photo_scaled[...] = photo_unit[...] * jnp.exp(warmth[...])


def normalize(warmth, photo, text):
    n, d = photo.shape
    vm = pl.BlockSpec(memory_space=pltpu.VMEM)
    full = jax.ShapeDtypeStruct((n, d), F32)
    one = jax.ShapeDtypeStruct((n, 1), F32)
    return pl.pallas_call(
        normalize_kernel,
        in_specs=[vm, vm, vm],
        out_specs=[vm] * 5,
        out_shape=[full, full, one, full, one],
    )(warmth.reshape(1, 1), photo, text)


def pairs_kernel(bases, shift, img, match, txt, gi, gt, ah, al, bh, bl, *, ti, tj, n):
    j = pl.program_id(0)
    rows_all = img.shape[0]

    @pl.when(j == 0)
    def _():
        gi[...] = jnp.zeros_like(gi)

        def split(i, c):
            rows = pl.ds(pl.multiple_of(i * n, n), n)
            ah[rows, :], al[rows, :] = halves(img[rows, :])
            return c

        lax.fori_loop(0, rows_all // n, split, 0)

    bh[...], bl[...] = halves(txt[...])
    gt[...] = jnp.zeros_like(gt)
    lane = lax.broadcasted_iota(jnp.int32, (1, n), 1)
    per = tj // n
    col = jnp.concatenate([lane + bases[j * per + q] for q in range(per)], axis=1)

    def step(i, c):
        rows = pl.ds(pl.multiple_of(i * ti, ti), ti)
        a_h = ah[rows, :]
        a_l = al[rows, :]
        b_h = bh[...]
        b_l = bl[...]
        s = mm(a_h, b_h, 1, 1) + mm(a_h, b_l, 1, 1) + mm(a_l, b_h, 1, 1)
        p = 1.0 / (1.0 + jnp.exp(-(s + shift[0])))
        p = jnp.where(match[rows, :] == col, p - 1.0, p)
        p_h, p_l = halves(p)
        gi[rows, :] += mm(p_h, b_h, 1, 0) + mm(p_h, b_l, 1, 0) + mm(p_l, b_h, 1, 0)
        gt[...] += mm(p_h, a_h, 0, 0) + mm(p_h, a_l, 0, 0) + mm(p_l, a_h, 0, 0)
        return c

    lax.fori_loop(0, rows_all // ti, step, 0)


def pair_gradients(bases, shift, img, match, txt, n, ti=512, tj=512):
    rows, d = img.shape
    cols = txt.shape[0]
    sm = pl.BlockSpec(memory_space=pltpu.SMEM)
    return pl.pallas_call(
        functools.partial(pairs_kernel, ti=ti, tj=tj, n=n),
        grid=(cols // tj,),
        in_specs=[
            sm,
            sm,
            pl.BlockSpec((rows, d), lambda j: (0, 0)),
            pl.BlockSpec((rows, 1), lambda j: (0, 0)),
            pl.BlockSpec((tj, d), lambda j: (j, 0)),
        ],
        out_specs=[pl.BlockSpec((rows, d), lambda j: (0, 0)), pl.BlockSpec((tj, d), lambda j: (j, 0))],
        out_shape=[jax.ShapeDtypeStruct((rows, d), F32), jax.ShapeDtypeStruct((cols, d), F32)],
        scratch_shapes=[pltpu.VMEM((rows, d), BF16)] * 2 + [pltpu.VMEM((tj, d), BF16)] * 2,
        compiler_params=pltpu.CompilerParams(vmem_limit_bytes=58 * 2**20),
        cost_estimate=pl.CostEstimate(
            flops=18 * rows * cols * d, bytes_accessed=8 * (rows + cols) * d, transcendentals=2 * rows * cols
        ),
    )(bases, shift, img, match, txt)


def gather_shares(own, ring, pair):
    half = own.shape[0] // 2
    back = shift_by(own, ring, 1)
    front = shift_by(own, ring, -1)
    twin = shift_by(own, pair, 1)
    twin_back = shift_by(twin, ring, 1)
    twin_front = shift_by(twin, ring, -1)
    far = jnp.concatenate([shift_by(back[:half], ring, 1), shift_by(front[half:], ring, -1)])
    twin_far = jnp.concatenate([shift_by(twin_back[:half], ring, 1), shift_by(twin_front[half:], ring, -1)])
    return [own, twin, back, front, twin_back, twin_front, far, twin_far]


def reduce_shares(parts, ring, pair):
    own, twin, back, front, twin_back, twin_front, far, twin_far = parts
    half = own.shape[0] // 2

    def relay(ahead, behind, farthest):
        up = shift_by(farthest[:half], ring, 1)
        down = shift_by(farthest[half:], ring, -1)
        ahead = jnp.concatenate([ahead[:half] + up, ahead[half:]])
        behind = jnp.concatenate([behind[:half], behind[half:] + down])
        return shift_by(ahead, ring, 1) + shift_by(behind, ring, -1)

    twin = twin + relay(twin_front, twin_back, twin_far)
    return own + relay(front, back, far) + shift_by(twin, pair, 1)


def restore(grad, unit, length):
    along = jnp.sum(unit * grad, axis=-1, keepdims=True)
    return (grad - unit * along) / length


def per_device(photo, text, matching_index, warmth, shift):
    n = photo.shape[0]
    yl, x, yh, z, c = (lax.axis_index(a) for a in AXES)
    nx, nz = lax.axis_size("x"), lax.axis_size("z")
    ncol = lax.axis_size("yh") * nz * 2
    photo_scaled, photo_unit, photo_len, text_unit, text_len = normalize(warmth, photo, text)

    imgs = gather_shares(photo_scaled, "x", "yl")
    txts = []
    for share in gather_shares(text_unit, "z", "yh"):
        txts += [share, shift_by(share, "c", 1)]

    col = (yh * nz + z) * 2 + c
    rows = [(yl ^ dy) * nx + (x + dx) % nx for dx, dy in PLACES]
    match = jnp.concatenate([lax.dynamic_slice(matching_index, ((r * ncol + col) * n,), (n,)) for r in rows])
    row = yl * nx + x
    cols = [((yh ^ dy) * nz + (z + dz) % nz) * 2 + (c ^ k) for dz, dy in PLACES for k in (0, 1)]
    bases = jnp.stack([(row * ncol + q) * n for q in cols]).astype(jnp.int32)

    gi, gt = pair_gradients(bases, shift, jnp.concatenate(imgs), match[:, None], jnp.concatenate(txts), n)
    gi = [gi[k * n : (k + 1) * n] for k in range(8)]
    gt = [gt[k * n : (k + 1) * n] for k in range(16)]
    photo_grad = reduce_shares(gi, "x", "yl") * jnp.exp(warmth)
    text_grad = reduce_shares([gt[2 * k] + shift_by(gt[2 * k + 1], "c", 1) for k in range(8)], "z", "yh")
    return restore(photo_grad, photo_unit, photo_len), restore(text_grad, text_unit, text_len)


def solution(mesh):
    fine = Mesh(mesh.devices.reshape(2, 4, 2, 4, 2), AXES)
    spec = P(AXES, None)
    return jax.shard_map(
        per_device,
        mesh=fine,
        in_specs=(spec, spec, P(), P(), P()),
        out_specs=(spec, spec),
        check_vma=False,
    )
```

```python
import functools

import jax
import jax.numpy as jnp
from jax import lax
from jax.experimental import pallas as pl
from jax.experimental.pallas import tpu as pltpu
from jax.sharding import Mesh
from jax.sharding import PartitionSpec as P

EPS = 1e-06
F32 = jnp.float32
BF16 = jnp.bfloat16
AXES = ("yl", "x", "yh", "z", "c")
PLACES = ((0, 0), (0, 1), (-1, 0), (1, 1), (2, 0), (2, 1), (1, 0), (-1, 1))


def shift_by(value, axis, steps):
    count = lax.axis_size(axis)
    return lax.ppermute(value, axis, [(i, (i + steps) % count) for i in range(count)])


def mm(a, b, ca, cb):
    return lax.dot_general(a, b, (((ca,), (cb,)), ((), ())), preferred_element_type=F32)


def halves(x):
    hi = x.astype(BF16)
    return hi, (x - hi.astype(F32)).astype(BF16)


def normalize_kernel(warmth, photo, text, photo_scaled, photo_unit, photo_len, text_unit, text_len):
    for raw, unit, length in ((photo, photo_unit, photo_len), (text, text_unit, text_len)):
        x = raw[...]
        size = jnp.sqrt(jnp.sum(x * x, axis=-1, keepdims=True) + EPS)
        unit[...] = x / size
        length[...] = size
    photo_scaled[...] = photo_unit[...] * jnp.exp(warmth[...])


def normalize(warmth, photo, text):
    n, d = photo.shape
    vm = pl.BlockSpec(memory_space=pltpu.VMEM)
    full = jax.ShapeDtypeStruct((n, d), F32)
    one = jax.ShapeDtypeStruct((n, 1), F32)
    return pl.pallas_call(
        normalize_kernel,
        in_specs=[vm, vm, vm],
        out_specs=[vm] * 5,
        out_shape=[full, full, one, full, one],
    )(warmth.reshape(1, 1), photo, text)


def pairs_kernel(bases, shift, match, *refs, shares, parts, n, ti, tj):
    imgs, refs = refs[:shares], refs[shares:]
    count = sum(len(p) for p in parts)
    txts, gi_out, gt_out = refs[:count], refs[count : count + shares], refs[count + shares : 2 * count + shares]
    gi, gt, raw, ah, al, bh, bl, img_in, img_out, txt_in, txt_out = refs[2 * count + shares :]
    j = pl.program_id(0)
    last = len(parts) - 1

    def text_copies(k, refs, buf, sems, out):
        row, copies = 0, []
        for i, q in enumerate(parts[k]):
            here = buf.at[k % 2, pl.ds(row, q[1])]
            there = refs[q[0]]
            sem = sems.at[k % 2, i]
            copies.append(pltpu.make_async_copy(here, there, sem) if out else pltpu.make_async_copy(there, here, sem))
            row += q[1]
        return copies

    def text_in(k):
        return text_copies(k, txts, raw, txt_in, False)

    def text_out(k):
        return text_copies(k, gt_out, gt, txt_out, True)

    @pl.when(j == 0)
    def _():
        copies = [pltpu.make_async_copy(imgs[k], gi.at[pl.ds(k * n, n)], img_in.at[k]) for k in range(shares)]
        for c in copies + text_in(0):
            c.start()
        for k, c in enumerate(copies):
            c.wait()
            rows = pl.ds(k * n, n)
            ah[rows, :], al[rows, :] = halves(gi[rows, :])
        gi[...] = jnp.zeros_like(gi)

    for k in range(last + 1):

        @pl.when(j == k)
        def _():
            if k < last:
                for c in text_in(k + 1):
                    c.start()
            for c in text_in(k):
                c.wait()
            if k >= 2:
                for c in text_out(k - 2):
                    c.wait()

    slot = j % 2
    bh[...], bl[...] = halves(raw[slot])
    gt[slot] = jnp.zeros((tj, gt.shape[2]), F32)
    lane = lax.broadcasted_iota(jnp.int32, (1, n), 1)
    per = tj // n
    col = jnp.concatenate([lane + bases[j * per + q] for q in range(per)], axis=1)

    def step(i, c):
        rows = pl.ds(pl.multiple_of(i * ti, ti), ti)
        a_h = ah[rows, :]
        a_l = al[rows, :]
        b_h = bh[...]
        b_l = bl[...]
        s = mm(a_h, b_h, 1, 1) + mm(a_h, b_l, 1, 1) + mm(a_l, b_h, 1, 1)
        p = 1.0 / (1.0 + jnp.exp(-(s + shift[0])))
        p = jnp.where(match[rows, :] == col, p - 1.0, p)
        p_h, p_l = halves(p)
        gi[rows, :] += mm(p_h, b_h, 1, 0) + mm(p_h, b_l, 1, 0) + mm(p_l, b_h, 1, 0)
        gt[slot] += mm(p_h, a_h, 0, 0) + mm(p_h, a_l, 0, 0) + mm(p_l, a_h, 0, 0)
        return c

    lax.fori_loop(0, shares * n // ti, step, 0)

    for k in range(last + 1):

        @pl.when(j == k)
        def _():
            for c in text_out(k):
                c.start()

    @pl.when(j == last)
    def _():
        copies = [pltpu.make_async_copy(gi.at[pl.ds(k * n, n)], gi_out[k], img_out.at[k]) for k in range(shares)]
        for c in copies:
            c.start()
        for c in copies + text_out(last - 1) + text_out(last):
            c.wait()


def pair_gradients(shift, imgs, match, txts, parts, bases, ti=512):
    n, d = imgs[0].shape
    rows, tj = len(imgs) * n, sum(q[1] for q in parts[0])
    cols = len(parts) * tj
    sm, vm, far = (pl.BlockSpec(memory_space=m) for m in (pltpu.SMEM, pltpu.VMEM, pl.ANY))
    out = [jax.ShapeDtypeStruct(x.shape, F32) for x in (*imgs, *txts)]
    out = pl.pallas_call(
        functools.partial(pairs_kernel, shares=len(imgs), parts=parts, n=n, ti=ti, tj=tj),
        grid=(len(parts),),
        in_specs=[sm, sm, vm] + [far] * len(out),
        out_specs=[far] * len(out),
        scratch_shapes=[pltpu.VMEM((rows, d), F32)]
        + [pltpu.VMEM((2, tj, d), F32)] * 2
        + [pltpu.VMEM((rows, d), BF16)] * 2
        + [pltpu.VMEM((tj, d), BF16)] * 2
        + [pltpu.SemaphoreType.DMA((len(imgs),))] * 2
        + [pltpu.SemaphoreType.DMA((2, 2))] * 2,
        out_shape=out,
        compiler_params=pltpu.CompilerParams(vmem_limit_bytes=58 * 2**20),
        cost_estimate=pl.CostEstimate(
            flops=18 * rows * cols * d, bytes_accessed=8 * (rows + cols) * d, transcendentals=2 * rows * cols
        ),
    )(bases, shift, match, *imgs, *txts)
    return out[: len(imgs)], out[len(imgs) :]


def gather_shares(photo, text):
    hold = lax.optimization_barrier
    ups, downs = [(photo, text)], []
    up, down = hold(
        (
            (shift_by(photo, "x", 1), shift_by(text, "z", 1)),
            (shift_by(photo, "yl", 1), shift_by(text, "yh", 1)),
        )
    )
    for hop in range(3):
        ups.append(up)
        downs.append(down)
        nxt = tuple(shift_by(v, a, -1) for v, a in zip(down, ("x", "z")))
        if hop < 2:
            up, down = hold((tuple(shift_by(v, a, 1) for v, a in zip(up, ("x", "z"))), nxt))
        else:
            downs.append(hold(nxt))
    return ([pair[k] for both in zip(ups, downs) for pair in both] for k in (0, 1))


def reduce_shares(photo, text_mine, text_other):
    hold = lax.optimization_barrier
    i_own, i_twin, i_back, i_twin_front, i_far, i_twin_far, i_front, i_twin_back = photo
    n = i_own.shape[0]

    def join(k, other):
        both = text_mine[k] + shift_by(other, "c", 1)
        return both[:n], both[n:]

    i_up, i_down = shift_by(i_far, "x", 1), shift_by(i_twin_far, "x", -1)
    t_far, t_twin_far = join(2, text_other[2])
    rest = (text_other[0], text_other[1], text_other[3])
    rest, t_far, t_twin_far = hold((rest, t_far, t_twin_far))
    t_up, t_down = shift_by(t_far, "z", 1), shift_by(t_twin_far, "z", -1)
    i_up, i_down, t_up, t_down = hold((i_up, i_down, t_up, t_down))
    t_back, t_twin_front = join(1, rest[1])
    t_front, t_twin_back = join(3, rest[2])
    i_p, i_q = shift_by(i_twin_front, "x", 1), shift_by(i_twin_back + i_down, "x", -1)
    near, t_up, t_down = hold((rest[0], t_up, t_down))
    t_own, t_twin = join(0, near)
    t_p, t_q = shift_by(t_twin_front, "z", 1), shift_by(t_twin_back + t_down, "z", -1)
    i_back, t_back, i_p, i_q = hold((i_back, t_back, i_p, i_q))
    i_y = shift_by(i_twin + i_p + i_q, "yl", 1)
    i_r, i_s = shift_by(i_front + i_up, "x", 1), shift_by(i_back, "x", -1)
    t_s = shift_by(t_back, "z", -1)
    t_front, t_p = hold((t_front + t_up, t_p))
    t_y = shift_by(t_twin + t_p + t_q, "yh", 1)
    t_r = shift_by(t_front, "z", 1)
    return i_own + i_r + i_s + i_y, t_own + t_r + t_s + t_y


def restore(grad, unit, length):
    along = jnp.sum(unit * grad, axis=-1, keepdims=True)
    return (grad - unit * along) / length


def per_device(photo, text, matching_index, warmth, shift):
    n = photo.shape[0]
    yl, x, yh, z, c = (lax.axis_index(a) for a in AXES)
    nx, nz = lax.axis_size("x"), lax.axis_size("z")
    ncol = lax.axis_size("yh") * nz * 2
    photo_scaled, photo_unit, photo_len, text_unit, text_len = normalize(warmth, photo, text)

    imgs, txts = gather_shares(photo_scaled, text_unit)
    txts = [jnp.concatenate(txts[k : k + 2]) for k in range(0, 8, 2)]
    txts = [t for own in txts for t in (own, shift_by(own, "c", 1))]
    parts = [((2 * k, 2 * n), (2 * k + 1, 2 * n)) for k in range(4)]

    col = (yh * nz + z) * 2 + c
    row = yl * nx + x
    places = [(yl ^ dy) * nx + (x + dx) % nx for dx, dy in PLACES]
    match = jnp.concatenate([lax.dynamic_slice(matching_index, ((r * ncol + col) * n,), (n,)) for r in places])
    match = match[:, None]
    mine, other = ([((yh ^ dy) * nz + (z + dz) % nz) * 2 + (c ^ k) for dz, dy in PLACES] for k in (0, 1))
    cols = [q for k in range(0, 8, 2) for q in mine[k : k + 2] + other[k : k + 2]]
    bases = jnp.stack([(row * ncol + q) * n for q in cols]).astype(jnp.int32)

    gi, gt = pair_gradients(shift, imgs, match, txts, parts, bases)
    photo_grad, text_grad = reduce_shares(gi, gt[0::2], gt[1::2])
    photo_grad = photo_grad * jnp.exp(warmth)
    return restore(photo_grad, photo_unit, photo_len), restore(text_grad, text_unit, text_len)


def solution(mesh):
    fine = Mesh(mesh.devices.reshape(2, 4, 2, 4, 2), AXES)
    spec = P(AXES, None)
    return jax.shard_map(
        per_device,
        mesh=fine,
        in_specs=(spec, spec, P(), P(), P()),
        out_specs=(spec, spec),
        check_vma=False,
    )
```

```python
import functools

import jax
import jax.numpy as jnp
from jax import lax
from jax.experimental import pallas as pl
from jax.experimental.pallas import tpu as pltpu
from jax.sharding import Mesh
from jax.sharding import PartitionSpec as P

EPS = 1e-06
F32 = jnp.float32
BF16 = jnp.bfloat16
AXES = ("yl", "x", "yh", "z", "c")
PLACES = ((0, 0), (0, 1), (-1, 0), (1, 0), (2, 0), (2, 1), (1, 1), (-1, 1))


def shift_by(value, axis, steps):
    count = lax.axis_size(axis)
    return lax.ppermute(value, axis, [(i, (i + steps) % count) for i in range(count)])


def mm(a, b, ca, cb):
    return lax.dot_general(a, b, (((ca,), (cb,)), ((), ())), preferred_element_type=F32)


def halves(x):
    hi = x.astype(BF16)
    return hi, (x - hi.astype(F32)).astype(BF16)


def normalize_kernel(warmth, photo, text, photo_scaled, photo_unit, photo_len, text_unit, text_len):
    for raw, unit, length in ((photo, photo_unit, photo_len), (text, text_unit, text_len)):
        x = raw[...]
        size = jnp.sqrt(jnp.sum(x * x, axis=-1, keepdims=True) + EPS)
        unit[...] = x / size
        length[...] = size
    photo_scaled[...] = photo_unit[...] * jnp.exp(warmth[...])


def normalize(warmth, photo, text):
    n, d = photo.shape
    vm = pl.BlockSpec(memory_space=pltpu.VMEM)
    full = jax.ShapeDtypeStruct((n, d), F32)
    one = jax.ShapeDtypeStruct((n, 1), F32)
    return pl.pallas_call(
        normalize_kernel,
        in_specs=[vm, vm, vm],
        out_specs=[vm] * 5,
        out_shape=[full, full, one, full, one],
    )(warmth.reshape(1, 1), photo, text)


def pairs_kernel(bases, shift, match, *refs, shares, parts, n, ti, tj, more):
    imgs, refs = refs[:shares], refs[shares:]
    gi_in, refs = refs[: shares * more], refs[shares * more :]
    count = sum(len(p) for p in parts)
    txts, gi_out, gt_out = refs[:count], refs[count : count + shares], refs[count + shares : 2 * count + shares]
    gi, gt, raw, ah, al, bh, bl, img_in, img_out, sum_in, txt_in, txt_out = refs[2 * count + shares :]
    j = pl.program_id(0)
    last = len(parts) - 1

    def text_copies(k, refs, buf, sems, out):
        row, copies = 0, []
        for i, q in enumerate(parts[k]):
            here = buf.at[k % 2, pl.ds(row, q[1])]
            there = refs[q[0]]
            sem = sems.at[k % 2, i]
            copies.append(pltpu.make_async_copy(here, there, sem) if out else pltpu.make_async_copy(there, here, sem))
            row += q[1]
        return copies

    def text_in(k):
        return text_copies(k, txts, raw, txt_in, False)

    def text_out(k):
        return text_copies(k, gt_out, gt, txt_out, True)

    @pl.when(j == 0)
    def _():
        per = tj // n
        copies = [
            pltpu.make_async_copy(imgs[k], gt.at[k // per, pl.ds(k % per * n, n)], img_in.at[k]) for k in range(shares)
        ]
        sums = [pltpu.make_async_copy(gi_in[k], gi.at[pl.ds(k * n, n)], sum_in.at[k]) for k in range(shares * more)]
        for c in copies + text_in(0) + sums:
            c.start()
        for k, c in enumerate(copies):
            c.wait()
            rows = pl.ds(k * n, n)
            ah[rows, :], al[rows, :] = halves(gt[k // per, pl.ds(k % per * n, n), :])
        for c in sums:
            c.wait()
        if not more:
            gi[...] = jnp.zeros_like(gi)

    for k in range(last + 1):

        @pl.when(j == k)
        def _():
            if k < last:
                for c in text_in(k + 1):
                    c.start()
            for c in text_in(k):
                c.wait()
            if k >= 2:
                for c in text_out(k - 2):
                    c.wait()

    slot = j % 2
    bh[...], bl[...] = halves(raw[slot])
    gt[slot] = jnp.zeros((tj, gt.shape[2]), F32)
    lane = lax.broadcasted_iota(jnp.int32, (1, n), 1)
    per = tj // n
    col = jnp.concatenate([lane + bases[j * per + q] for q in range(per)], axis=1)

    def step(i, c):
        rows = pl.ds(pl.multiple_of(i * ti, ti), ti)
        a_h = ah[rows, :]
        a_l = al[rows, :]
        b_h = bh[...]
        b_l = bl[...]
        s = mm(a_h, b_h, 1, 1) + mm(a_h, b_l, 1, 1) + mm(a_l, b_h, 1, 1)
        p = 1.0 / (1.0 + jnp.exp(-(s + shift[0])))
        p = jnp.where(match[rows, :] == col, p - 1.0, p)
        p_h, p_l = halves(p)
        gi[rows, :] += mm(p_h, b_h, 1, 0) + mm(p_h, b_l, 1, 0) + mm(p_l, b_h, 1, 0)
        gt[slot] += mm(p_h, a_h, 0, 0) + mm(p_h, a_l, 0, 0) + mm(p_l, a_h, 0, 0)
        return c

    lax.fori_loop(0, shares * n // ti, step, 0)

    for k in range(last + 1):

        @pl.when(j == k)
        def _():
            for c in text_out(k):
                c.start()

    @pl.when(j == last)
    def _():
        copies = [pltpu.make_async_copy(gi.at[pl.ds(k * n, n)], gi_out[k], img_out.at[k]) for k in range(shares)]
        for c in copies:
            c.start()
        for c in copies + text_out(last - 1) + text_out(last):
            c.wait()


def pair_gradients(shift, imgs, match, txts, parts, bases, sums=(), ti=512):
    n, d = imgs[0].shape
    rows, tj = len(imgs) * n, sum(q[1] for q in parts[0])
    cols = len(parts) * tj
    sm, vm, far = (pl.BlockSpec(memory_space=m) for m in (pltpu.SMEM, pltpu.VMEM, pl.ANY))
    out = [jax.ShapeDtypeStruct(x.shape, F32) for x in (*imgs, *txts)]
    out = pl.pallas_call(
        functools.partial(pairs_kernel, shares=len(imgs), parts=parts, n=n, ti=ti, tj=tj, more=int(len(sums) > 0)),
        grid=(len(parts),),
        in_specs=[sm, sm, vm] + [far] * (len(out) + len(sums)),
        out_specs=[far] * len(out),
        scratch_shapes=[pltpu.VMEM((rows, d), F32)]
        + [pltpu.VMEM((2, tj, d), F32)] * 2
        + [pltpu.VMEM((rows, d), BF16)] * 2
        + [pltpu.VMEM((tj, d), BF16)] * 2
        + [pltpu.SemaphoreType.DMA((len(imgs),))] * 3
        + [pltpu.SemaphoreType.DMA((2, 2))] * 2,
        out_shape=out,
        compiler_params=pltpu.CompilerParams(vmem_limit_bytes=58 * 2**20),
        cost_estimate=pl.CostEstimate(
            flops=18 * rows * cols * d, bytes_accessed=8 * (rows + cols) * d, transcendentals=2 * rows * cols
        ),
    )(bases, shift, match, *imgs, *sums, *txts)
    return out[: len(imgs)], out[len(imgs) :]


def gather_shares(photo, text, index):
    hold = lax.optimization_barrier
    i_back, i_front = shift_by(photo, "x", 1), shift_by(photo, "x", -1)
    t_back, t_front = shift_by(text, "z", 1), shift_by(text, "z", -1)
    i_twin = shift_by(photo, "yl", 1)
    i_back, i_front, t_back, t_front, i_twin, text, index = hold((i_back, i_front, t_back, t_front, i_twin, text, index))
    t_twin = shift_by(text, "yh", 1)
    i_far, t_far = shift_by(i_back, "x", 1), shift_by(t_back, "z", 1)
    i_twin_front = shift_by(i_twin, "x", -1)
    t_twin, i_far, t_far, i_twin_front, i_twin = hold((t_twin, i_far, t_far, i_twin_front, i_twin))
    t_twin_front, t_twin_back = shift_by(t_twin, "z", -1), shift_by(t_twin, "z", 1)
    i_twin_far, i_twin_back = shift_by(i_twin_front, "x", -1), shift_by(i_twin, "x", 1)
    t_twin_front, t_twin_back, i_twin_far, i_twin_back = hold((t_twin_front, t_twin_back, i_twin_far, i_twin_back))
    t_twin_far = shift_by(t_twin_front, "z", -1)
    imgs = [photo, i_twin, i_back, i_front, i_far, i_twin_far, i_twin_front, i_twin_back]
    txts = [text, t_twin, t_back, t_front, t_far, t_twin_far, t_twin_front, t_twin_back]
    return imgs, txts, index


def split_rows(x, n):
    return [x[k : k + n] for k in range(0, x.shape[0], n)]


def reduce_shares(photo, text_near, text_far):
    hold = lax.optimization_barrier
    i_own, i_twin, i_back, i_front, i_far, i_twin_far, i_twin_front, i_twin_back = photo
    n = i_own.shape[0]
    i_up, i_down = shift_by(i_far, "x", 1), shift_by(i_twin_far, "x", -1)
    near, far = shift_by(text_near[1], "c", 1), text_far[1]
    near, far = hold((near, far))
    t_far, t_twin_far, t_twin_front, t_twin_back = split_rows(text_far[0] + shift_by(far, "c", 1), n)
    t_up, t_down = shift_by(t_far, "z", 1), shift_by(t_twin_far, "z", -1)
    t_own, t_twin, t_back, t_front = split_rows(text_near[0] + near, n)
    i_up, i_down, t_up, t_down, t_back = hold((i_up, i_down, t_up, t_down, t_back))
    i_p, i_q = shift_by(i_twin_front, "x", 1), shift_by(i_twin_back + i_down, "x", -1)
    t_p, t_q = shift_by(t_twin_front, "z", 1), shift_by(t_twin_back + t_down, "z", -1)
    t_s = shift_by(t_back, "z", -1)
    i_back, i_p, i_q, t_p, t_q = hold((i_back, i_p, i_q, t_p, t_q))
    i_y = shift_by(i_twin + i_p + i_q, "yl", 1)
    t_y = shift_by(t_twin + t_p + t_q, "yh", 1)
    i_r, i_s = shift_by(i_front + i_up, "x", 1), shift_by(i_back, "x", -1)
    t_r = shift_by(t_front + t_up, "z", 1)
    return i_own + i_r + i_s + i_y, t_own + t_r + t_s + t_y


def restore(grad, unit, length):
    along = jnp.sum(unit * grad, axis=-1, keepdims=True)
    return (grad - unit * along) / length


def per_device(photo, text, matching_index, warmth, shift):
    n = photo.shape[0]
    yl, x, yh, z, c = (lax.axis_index(a) for a in AXES)
    nx, nz = lax.axis_size("x"), lax.axis_size("z")
    ncol = lax.axis_size("yh") * nz * 2
    photo_scaled, photo_unit, photo_len, text_unit, text_len = normalize(warmth, photo, text)

    col = (yh * nz + z) * 2 + c
    row = yl * nx + x
    places = [(yl ^ dy) * nx + (x + dx) % nx for dx, dy in PLACES]
    match = jnp.concatenate([lax.dynamic_slice(matching_index, ((r * ncol + col) * n,), (n,)) for r in places])
    mine, other = ([((yh ^ dy) * nz + (z + dz) % nz) * 2 + (c ^ k) for dz, dy in PLACES] for k in (0, 1))
    cols = mine[:4] + other[:4] + mine[4:] + other[4:]
    bases = jnp.stack([(row * ncol + q) * n for q in cols]).astype(jnp.int32)

    imgs, txts, (match, bases) = gather_shares(photo_scaled, text_unit, (match[:, None], bases))
    near = jnp.concatenate(txts[:4])
    near = (near, shift_by(near, "c", 1))
    parts = [((k, 4 * n),) for k in (0, 1)]
    gi, gt_near = pair_gradients(shift, imgs, match, near, parts, bases[:8])
    gi, last = lax.optimization_barrier((gi, txts[5]))
    far = jnp.concatenate([txts[4], last, *txts[6:]])
    far = (far, shift_by(far, "c", 1))
    gi, gt_far = pair_gradients(shift, imgs, match, far, parts, bases[8:], sums=gi)
    photo_grad, text_grad = reduce_shares(gi, gt_near, gt_far)
    photo_grad = photo_grad * jnp.exp(warmth)
    return restore(photo_grad, photo_unit, photo_len), restore(text_grad, text_unit, text_len)


def solution(mesh):
    fine = Mesh(mesh.devices.reshape(2, 4, 2, 4, 2), AXES)
    spec = P(AXES, None)
    return jax.shard_map(
        per_device,
        mesh=fine,
        in_specs=(spec, spec, P(), P(), P()),
        out_specs=(spec, spec),
        check_vma=False,
    )
```

```python
import functools

import jax
import jax.numpy as jnp
from jax import lax
from jax.experimental import pallas as pl
from jax.experimental.pallas import tpu as pltpu
from jax.sharding import Mesh
from jax.sharding import PartitionSpec as P

EPS = 1e-06
F32 = jnp.float32
BF16 = jnp.bfloat16
F8 = jnp.float8_e4m3fn
P_HI, P_LO = 2.0**8, 2.0**17
TXT_HI, TXT_LO = 2.0**8, 2.0**17
IMG_HI, IMG_LO = 2.0**1, 2.0**10
AXES = ("yl", "x", "yh", "z", "c")
PLACES = ((0, 0), (0, 1), (-1, 0), (1, 0), (2, 0), (2, 1), (1, 1), (-1, 1))


def shift_by(value, axis, steps):
    count = lax.axis_size(axis)
    return lax.ppermute(value, axis, [(i, (i + steps) % count) for i in range(count)])


def mm(a, b, ca, cb):
    return lax.dot_general(a, b, (((ca,), (cb,)), ((), ())), preferred_element_type=F32)


def halves(x):
    hi = x.astype(BF16)
    return hi, (x - hi.astype(F32)).astype(BF16)


def eighths(hi, lo, hi_scale, lo_scale):
    return (hi.astype(F32) * hi_scale).astype(F8), (lo.astype(F32) * lo_scale).astype(F8)


def normalize_kernel(warmth, photo, text, photo_scaled, photo_unit, photo_len, text_unit, text_len):
    for raw, unit, length in ((photo, photo_unit, photo_len), (text, text_unit, text_len)):
        x = raw[...]
        size = jnp.sqrt(jnp.sum(x * x, axis=-1, keepdims=True) + EPS)
        unit[...] = x / size
        length[...] = size
    photo_scaled[...] = photo_unit[...] * jnp.exp(warmth[...])


def normalize(warmth, photo, text):
    n, d = photo.shape
    vm = pl.BlockSpec(memory_space=pltpu.VMEM)
    full = jax.ShapeDtypeStruct((n, d), F32)
    one = jax.ShapeDtypeStruct((n, 1), F32)
    return pl.pallas_call(
        normalize_kernel,
        in_specs=[vm, vm, vm],
        out_specs=[vm] * 5,
        out_shape=[full, full, one, full, one],
    )(warmth.reshape(1, 1), photo, text)


def pairs_kernel(bases, shift, match, *refs, shares, parts, n, ti, tj, more):
    imgs, refs = refs[:shares], refs[shares:]
    gi_in, refs = refs[: shares * more], refs[shares * more :]
    count = sum(len(p) for p in parts)
    txts, gi_out, gt_out = refs[:count], refs[count : count + shares], refs[count + shares : 2 * count + shares]
    gi, gt, raw, ah, al, bh, bl, ah8, al8, bh8, bl8, img_in, img_out, sum_in, txt_in, txt_out = refs[2 * count + shares :]
    j = pl.program_id(0)
    last = len(parts) - 1

    def text_copies(k, refs, buf, sems, out):
        row, copies = 0, []
        for i, q in enumerate(parts[k]):
            here = buf.at[k % 2, pl.ds(row, q[1])]
            there = refs[q[0]]
            sem = sems.at[k % 2, i]
            copies.append(pltpu.make_async_copy(here, there, sem) if out else pltpu.make_async_copy(there, here, sem))
            row += q[1]
        return copies

    def text_in(k):
        return text_copies(k, txts, raw, txt_in, False)

    def text_out(k):
        return text_copies(k, gt_out, gt, txt_out, True)

    @pl.when(j == 0)
    def _():
        per = tj // n
        copies = [
            pltpu.make_async_copy(imgs[k], gt.at[k // per, pl.ds(k % per * n, n)], img_in.at[k]) for k in range(shares)
        ]
        sums = [pltpu.make_async_copy(gi_in[k], gi.at[pl.ds(k * n, n)], sum_in.at[k]) for k in range(shares * more)]
        for c in copies + text_in(0) + sums:
            c.start()
        for k, c in enumerate(copies):
            c.wait()
            rows = pl.ds(k * n, n)
            hi, lo = halves(gt[k // per, pl.ds(k % per * n, n), :])
            ah[rows, :], al[rows, :] = hi, lo
            ah8[rows, :], al8[rows, :] = eighths(hi, lo, IMG_HI, IMG_LO)
        for c in sums:
            c.wait()
        if not more:
            gi[...] = jnp.zeros_like(gi)

    for k in range(last + 1):

        @pl.when(j == k)
        def _():
            if k < last:
                for c in text_in(k + 1):
                    c.start()
            for c in text_in(k):
                c.wait()
            if k >= 2:
                for c in text_out(k - 2):
                    c.wait()

    slot = j % 2
    hi, lo = halves(raw[slot])
    bh[...], bl[...] = hi, lo
    bh8[...], bl8[...] = eighths(hi, lo, TXT_HI, TXT_LO)
    gt[slot] = jnp.zeros((tj, gt.shape[2]), F32)
    lane = lax.broadcasted_iota(jnp.int32, (1, n), 1)
    per = tj // n
    col = jnp.concatenate([lane + bases[j * per + q] for q in range(per)], axis=1)

    def step(i, c):
        rows = pl.ds(pl.multiple_of(i * ti, ti), ti)
        a_h = ah[rows, :]
        a_l = al[rows, :]
        b_h = bh[...]
        b_l = bl[...]
        s = mm(a_h, b_h, 1, 1) + mm(a_h, b_l, 1, 1) + mm(a_l, b_h, 1, 1)
        p = 1.0 / (1.0 + jnp.exp(-(s + shift[0])))
        p = jnp.where(match[rows, :] == col, p - 1.0, p)
        p_h, p_l = halves(p)
        p_h8, p_l8 = eighths(p_h, p_l, P_HI, P_LO)
        cross = mm(p_h8, bl8[...], 1, 0) + mm(p_l8, bh8[...], 1, 0)
        gi[rows, :] += mm(p_h, b_h, 1, 0) + cross * (1.0 / (P_HI * TXT_LO))
        cross = mm(p_h8, al8[rows, :], 0, 0) + mm(p_l8, ah8[rows, :], 0, 0)
        gt[slot] += mm(p_h, a_h, 0, 0) + cross * (1.0 / (P_HI * IMG_LO))
        return c

    lax.fori_loop(0, shares * n // ti, step, 0)

    for k in range(last + 1):

        @pl.when(j == k)
        def _():
            for c in text_out(k):
                c.start()

    @pl.when(j == last)
    def _():
        copies = [pltpu.make_async_copy(gi.at[pl.ds(k * n, n)], gi_out[k], img_out.at[k]) for k in range(shares)]
        for c in copies:
            c.start()
        for c in copies + text_out(last - 1) + text_out(last):
            c.wait()


def pair_gradients(shift, imgs, match, txts, parts, bases, sums=(), ti=1024):
    n, d = imgs[0].shape
    rows, tj = len(imgs) * n, sum(q[1] for q in parts[0])
    cols = len(parts) * tj
    sm, vm, far = (pl.BlockSpec(memory_space=m) for m in (pltpu.SMEM, pltpu.VMEM, pl.ANY))
    out = [jax.ShapeDtypeStruct(x.shape, F32) for x in (*imgs, *txts)]
    out = pl.pallas_call(
        functools.partial(pairs_kernel, shares=len(imgs), parts=parts, n=n, ti=ti, tj=tj, more=int(len(sums) > 0)),
        grid=(len(parts),),
        in_specs=[sm, sm, vm] + [far] * (len(out) + len(sums)),
        out_specs=[far] * len(out),
        scratch_shapes=[pltpu.VMEM((rows, d), F32)]
        + [pltpu.VMEM((2, tj, d), F32)] * 2
        + [pltpu.VMEM((rows, d), BF16)] * 2
        + [pltpu.VMEM((tj, d), BF16)] * 2
        + [pltpu.VMEM((rows, d), F8)] * 2
        + [pltpu.VMEM((tj, d), F8)] * 2
        + [pltpu.SemaphoreType.DMA((len(imgs),))] * 3
        + [pltpu.SemaphoreType.DMA((2, 2))] * 2,
        out_shape=out,
        compiler_params=pltpu.CompilerParams(vmem_limit_bytes=58 * 2**20),
        cost_estimate=pl.CostEstimate(
            flops=18 * rows * cols * d, bytes_accessed=8 * (rows + cols) * d, transcendentals=2 * rows * cols
        ),
    )(bases, shift, match, *imgs, *sums, *txts)
    return out[: len(imgs)], out[len(imgs) :]


def gather_shares(photo, text, index):
    hold = lax.optimization_barrier
    i_back, i_front = shift_by(photo, "x", 1), shift_by(photo, "x", -1)
    t_back, t_front = shift_by(text, "z", 1), shift_by(text, "z", -1)
    i_twin = shift_by(photo, "yl", 1)
    i_back, i_front, t_back, t_front, i_twin, text, index = hold((i_back, i_front, t_back, t_front, i_twin, text, index))
    t_twin = shift_by(text, "yh", 1)
    i_far, t_far = shift_by(i_back, "x", 1), shift_by(t_back, "z", 1)
    i_twin_front = shift_by(i_twin, "x", -1)
    t_twin, i_far, t_far, i_twin_front, i_twin = hold((t_twin, i_far, t_far, i_twin_front, i_twin))
    t_twin_front, t_twin_back = shift_by(t_twin, "z", -1), shift_by(t_twin, "z", 1)
    i_twin_far, i_twin_back = shift_by(i_twin_front, "x", -1), shift_by(i_twin, "x", 1)
    t_twin_front, t_twin_back, i_twin_far, i_twin_back = hold((t_twin_front, t_twin_back, i_twin_far, i_twin_back))
    t_twin_far = shift_by(t_twin_front, "z", -1)
    imgs = [photo, i_twin, i_back, i_front, i_far, i_twin_far, i_twin_front, i_twin_back]
    txts = [text, t_twin, t_back, t_front, t_far, t_twin_far, t_twin_front, t_twin_back]
    return imgs, txts, index


def split_rows(x, n):
    return [x[k : k + n] for k in range(0, x.shape[0], n)]


def reduce_shares(photo, text_near, text_far):
    hold = lax.optimization_barrier
    i_own, i_twin, i_back, i_front, i_far, i_twin_far, i_twin_front, i_twin_back = photo
    n = i_own.shape[0]
    i_up, i_down = shift_by(i_far, "x", 1), shift_by(i_twin_far, "x", -1)
    near, far = shift_by(text_near[1], "c", 1), text_far[1]
    near, far = hold((near, far))
    t_far, t_twin_far, t_twin_front, t_twin_back = split_rows(text_far[0] + shift_by(far, "c", 1), n)
    t_up, t_down = shift_by(t_far, "z", 1), shift_by(t_twin_far, "z", -1)
    t_own, t_twin, t_back, t_front = split_rows(text_near[0] + near, n)
    i_up, i_down, t_up, t_down, t_back = hold((i_up, i_down, t_up, t_down, t_back))
    i_p, i_q = shift_by(i_twin_front, "x", 1), shift_by(i_twin_back + i_down, "x", -1)
    t_p, t_q = shift_by(t_twin_front, "z", 1), shift_by(t_twin_back + t_down, "z", -1)
    t_s = shift_by(t_back, "z", -1)
    i_back, i_p, i_q = hold((i_back, i_p, i_q))
    i_y = shift_by(i_twin + i_p + i_q, "yl", 1)
    t_front, t_p, t_q = hold((t_front + t_up, t_p, t_q))
    t_y = shift_by(t_twin + t_p + t_q, "yh", 1)
    i_r, i_s = shift_by(i_front + i_up, "x", 1), shift_by(i_back, "x", -1)
    t_r = shift_by(t_front, "z", 1)
    return i_own + i_r + i_s + i_y, t_own + t_r + t_s + t_y


def restore(grad, unit, length):
    along = jnp.sum(unit * grad, axis=-1, keepdims=True)
    return (grad - unit * along) / length


def per_device(photo, text, matching_index, warmth, shift):
    n = photo.shape[0]
    yl, x, yh, z, c = (lax.axis_index(a) for a in AXES)
    nx, nz = lax.axis_size("x"), lax.axis_size("z")
    ncol = lax.axis_size("yh") * nz * 2
    photo_scaled, photo_unit, photo_len, text_unit, text_len = normalize(warmth, photo, text)

    col = (yh * nz + z) * 2 + c
    row = yl * nx + x
    places = [(yl ^ dy) * nx + (x + dx) % nx for dx, dy in PLACES]
    match = jnp.concatenate([lax.dynamic_slice(matching_index, ((r * ncol + col) * n,), (n,)) for r in places])
    mine, other = ([((yh ^ dy) * nz + (z + dz) % nz) * 2 + (c ^ k) for dz, dy in PLACES] for k in (0, 1))
    cols = mine[:4] + other[:4] + mine[4:] + other[4:]
    bases = jnp.stack([(row * ncol + q) * n for q in cols]).astype(jnp.int32)

    imgs, txts, (match, bases) = gather_shares(photo_scaled, text_unit, (match[:, None], bases))
    near = jnp.concatenate(txts[:4])
    near = (near, shift_by(near, "c", 1))
    parts = [((k, 4 * n),) for k in (0, 1)]
    gi, gt_near = pair_gradients(shift, imgs, match, near, parts, bases[:8])
    gi, last = lax.optimization_barrier((gi, txts[5]))
    far = jnp.concatenate([txts[4], last, *txts[6:]])
    far = (far, shift_by(far, "c", 1))
    gi, gt_far = pair_gradients(shift, imgs, match, far, parts, bases[8:], sums=gi)
    photo_grad, text_grad = reduce_shares(gi, gt_near, gt_far)
    photo_grad = photo_grad * jnp.exp(warmth)
    return restore(photo_grad, photo_unit, photo_len), restore(text_grad, text_unit, text_len)


def solution(mesh):
    fine = Mesh(mesh.devices.reshape(2, 4, 2, 4, 2), AXES)
    spec = P(AXES, None)
    return jax.shard_map(
        per_device,
        mesh=fine,
        in_specs=(spec, spec, P(), P(), P()),
        out_specs=(spec, spec),
        check_vma=False,
    )
```

```python
import functools

import jax
import jax.numpy as jnp
from jax import lax
from jax.experimental import pallas as pl
from jax.experimental.pallas import tpu as pltpu
from jax.sharding import Mesh
from jax.sharding import PartitionSpec as P

EPS = 1e-06
F32 = jnp.float32
BF16 = jnp.bfloat16
F8 = jnp.float8_e4m3fn
P_HI, P_LO = 2.0**8, 2.0**17
TXT_HI, TXT_LO = 2.0**8, 2.0**17
IMG_HI, IMG_LO = 2.0**1, 2.0**10
AXES = ("yl", "x", "yh", "z", "c")
PLACES = ((0, 0), (0, 1), (-1, 0), (1, 0), (2, 0), (2, 1), (1, 1), (-1, 1))


def shift_by(value, axis, steps):
    count = lax.axis_size(axis)
    return lax.ppermute(value, axis, [(i, (i + steps) % count) for i in range(count)])


def mm(a, b, ca, cb):
    return lax.dot_general(a, b, (((ca,), (cb,)), ((), ())), preferred_element_type=F32)


def halves(x):
    hi = x.astype(BF16)
    return hi, (x - hi.astype(F32)).astype(BF16)


def eighths(hi, lo, hi_scale, lo_scale):
    return (hi.astype(F32) * hi_scale).astype(F8), (lo.astype(F32) * lo_scale).astype(F8)


def normalize_kernel(warmth, photo, text, photo_scaled, photo_unit, photo_len, text_unit, text_len):
    for raw, unit, length in ((photo, photo_unit, photo_len), (text, text_unit, text_len)):
        x = raw[...]
        size = jnp.sqrt(jnp.sum(x * x, axis=-1, keepdims=True) + EPS)
        unit[...] = x / size
        length[...] = size
    photo_scaled[...] = photo_unit[...] * jnp.exp(warmth[...])


def normalize(warmth, photo, text):
    n, d = photo.shape
    vm = pl.BlockSpec(memory_space=pltpu.VMEM)
    full = jax.ShapeDtypeStruct((n, d), F32)
    one = jax.ShapeDtypeStruct((n, 1), F32)
    return pl.pallas_call(
        normalize_kernel,
        in_specs=[vm, vm, vm],
        out_specs=[vm] * 5,
        out_shape=[full, full, one, full, one],
    )(warmth.reshape(1, 1), photo, text)


def pairs_kernel(bases, shift, match, *refs, shares, parts, n, ti, tj, more):
    imgs, refs = refs[:shares], refs[shares:]
    gi_in, refs = refs[: shares * more], refs[shares * more :]
    count = sum(len(p) for p in parts)
    txts, gi_out, gt_out = refs[:count], refs[count : count + shares], refs[count + shares : 2 * count + shares]
    gi, gt, raw, ah, al, bh, bl, ah8, al8, bh8, bl8, img_in, img_out, sum_in, txt_in, txt_out = refs[2 * count + shares :]
    j = pl.program_id(0)
    last = len(parts) - 1

    def text_copies(k, refs, buf, sems, out):
        row, copies = 0, []
        for i, q in enumerate(parts[k]):
            here = buf.at[k % 2, pl.ds(row, q[1])]
            there = refs[q[0]]
            sem = sems.at[k % 2, i]
            copies.append(pltpu.make_async_copy(here, there, sem) if out else pltpu.make_async_copy(there, here, sem))
            row += q[1]
        return copies

    def text_in(k):
        return text_copies(k, txts, raw, txt_in, False)

    def text_out(k):
        return text_copies(k, gt_out, gt, txt_out, True)

    @pl.when(j == 0)
    def _():
        per = tj // n
        copies = [
            pltpu.make_async_copy(imgs[k], gt.at[k // per, pl.ds(k % per * n, n)], img_in.at[k]) for k in range(shares)
        ]
        sums = [pltpu.make_async_copy(gi_in[k], gi.at[pl.ds(k * n, n)], sum_in.at[k]) for k in range(shares * more)]
        for c in copies + text_in(0) + sums:
            c.start()
        for k, c in enumerate(copies):
            c.wait()
            rows = pl.ds(k * n, n)
            hi, lo = halves(gt[k // per, pl.ds(k % per * n, n), :])
            ah[rows, :], al[rows, :] = hi, lo
            ah8[rows, :], al8[rows, :] = eighths(hi, lo, IMG_HI, IMG_LO)
        for c in sums:
            c.wait()
        if not more:
            gi[...] = jnp.zeros_like(gi)

    for k in range(last + 1):

        @pl.when(j == k)
        def _():
            if k < last:
                for c in text_in(k + 1):
                    c.start()
            for c in text_in(k):
                c.wait()
            if k >= 2:
                for c in text_out(k - 2):
                    c.wait()

    slot = j % 2
    hi, lo = halves(raw[slot])
    bh[...], bl[...] = hi, lo
    bh8[...], bl8[...] = eighths(hi, lo, TXT_HI, TXT_LO)
    gt[slot] = jnp.zeros((tj, gt.shape[2]), F32)
    lane = lax.broadcasted_iota(jnp.int32, (1, n), 1)
    per = tj // n
    col = jnp.concatenate([lane + bases[j * per + q] for q in range(per)], axis=1)

    def step(i, c):
        rows = pl.ds(pl.multiple_of(i * ti, ti), ti)
        a_h = ah[rows, :]
        a_l = al[rows, :]
        b_h = bh[...]
        b_l = bl[...]
        s = mm(a_h, b_h, 1, 1) + mm(a_h, b_l, 1, 1) + mm(a_l, b_h, 1, 1)
        p = 1.0 / (1.0 + jnp.exp(-(s + shift[0])))
        p = jnp.where(match[rows, :] == col, p - 1.0, p)
        p_h, p_l = halves(p)
        p_h8, p_l8 = eighths(p_h, p_l, P_HI, P_LO)
        cross = mm(p_h8, bl8[...], 1, 0) + mm(p_l8, bh8[...], 1, 0)
        gi[rows, :] += mm(p_h, b_h, 1, 0) + cross * (1.0 / (P_HI * TXT_LO))
        cross = mm(p_h8, al8[rows, :], 0, 0) + mm(p_l8, ah8[rows, :], 0, 0)
        gt[slot] += mm(p_h, a_h, 0, 0) + cross * (1.0 / (P_HI * IMG_LO))
        return c

    lax.fori_loop(0, shares * n // ti, step, 0)

    for k in range(last + 1):

        @pl.when(j == k)
        def _():
            for c in text_out(k):
                c.start()

    @pl.when(j == last)
    def _():
        copies = [pltpu.make_async_copy(gi.at[pl.ds(k * n, n)], gi_out[k], img_out.at[k]) for k in range(shares)]
        for c in copies:
            c.start()
        for c in copies + text_out(last - 1) + text_out(last):
            c.wait()


def pair_gradients(shift, imgs, match, txts, parts, bases, sums=()):
    n, d = imgs[0].shape
    rows, tj = len(imgs) * n, sum(q[1] for q in parts[0])
    cols = len(parts) * tj
    sm, vm, far = (pl.BlockSpec(memory_space=m) for m in (pltpu.SMEM, pltpu.VMEM, pl.ANY))
    out = [jax.ShapeDtypeStruct(x.shape, F32) for x in (*imgs, *txts)]
    out = pl.pallas_call(
        functools.partial(pairs_kernel, shares=len(imgs), parts=parts, n=n, ti=rows, tj=tj, more=int(len(sums) > 0)),
        grid=(len(parts),),
        in_specs=[sm, sm, vm] + [far] * (len(out) + len(sums)),
        out_specs=[far] * len(out),
        scratch_shapes=[pltpu.VMEM((rows, d), F32)]
        + [pltpu.VMEM((2, tj, d), F32)] * 2
        + [pltpu.VMEM((rows, d), BF16)] * 2
        + [pltpu.VMEM((tj, d), BF16)] * 2
        + [pltpu.VMEM((rows, d), F8)] * 2
        + [pltpu.VMEM((tj, d), F8)] * 2
        + [pltpu.SemaphoreType.DMA((len(imgs),))] * 3
        + [pltpu.SemaphoreType.DMA((2, 2))] * 2,
        out_shape=out,
        compiler_params=pltpu.CompilerParams(vmem_limit_bytes=58 * 2**20),
        cost_estimate=pl.CostEstimate(
            flops=18 * rows * cols * d, bytes_accessed=8 * (rows + cols) * d, transcendentals=2 * rows * cols
        ),
    )(bases, shift, match, *imgs, *sums, *txts)
    return out[: len(imgs)], out[len(imgs) :]


def gather_shares(photo, text, index):
    hold = lax.optimization_barrier
    i_back, i_front = shift_by(photo, "x", 1), shift_by(photo, "x", -1)
    t_back, t_front = shift_by(text, "z", 1), shift_by(text, "z", -1)
    i_twin = shift_by(photo, "yl", 1)
    i_back, i_front, t_back, t_front, i_twin, text, index = hold((i_back, i_front, t_back, t_front, i_twin, text, index))
    t_twin = shift_by(text, "yh", 1)
    i_far, t_far = shift_by(i_back, "x", 1), shift_by(t_back, "z", 1)
    i_twin_front = shift_by(i_twin, "x", -1)
    t_twin, i_far, t_far, i_twin_front, i_twin = hold((t_twin, i_far, t_far, i_twin_front, i_twin))
    t_twin_front, t_twin_back = shift_by(t_twin, "z", -1), shift_by(t_twin, "z", 1)
    i_twin_far, i_twin_back = shift_by(i_twin_front, "x", -1), shift_by(i_twin, "x", 1)
    near = [photo, i_twin, i_back, i_front], [text, t_twin, t_back, t_front]
    return near, [i_far, i_twin_far, i_twin_front, i_twin_back], [t_far, t_twin_front, t_twin_back], index


def split_rows(x, n):
    return [x[k : k + n] for k in range(0, x.shape[0], n)]


def reduce_shares(photo, text_near, text_far):
    hold = lax.optimization_barrier
    i_own, i_twin, i_back, i_front, i_far, i_twin_far, i_twin_front, i_twin_back = photo
    n = i_own.shape[0]
    i_up, i_down = shift_by(i_far, "x", 1), shift_by(i_twin_far, "x", -1)
    near, far = shift_by(text_near[1], "c", 1), text_far[1]
    near, far = hold((near, far))
    t_far, t_twin_far, t_twin_front, t_twin_back = split_rows(text_far[0] + shift_by(far, "c", 1), n)
    t_up, t_down = shift_by(t_far, "z", 1), shift_by(t_twin_far, "z", -1)
    t_own, t_twin, t_back, t_front = split_rows(text_near[0] + near, n)
    i_up, i_down, t_up, t_down, t_back = hold((i_up, i_down, t_up, t_down, t_back))
    i_p, i_q = shift_by(i_twin_front, "x", 1), shift_by(i_twin_back + i_down, "x", -1)
    t_p, t_q = shift_by(t_twin_front, "z", 1), shift_by(t_twin_back + t_down, "z", -1)
    t_s = shift_by(t_back, "z", -1)
    i_back, i_p, i_q = hold((i_back, i_p, i_q))
    i_y = shift_by(i_twin + i_p + i_q, "yl", 1)
    t_front, t_p, t_q = hold((t_front + t_up, t_p, t_q))
    t_y = shift_by(t_twin + t_p + t_q, "yh", 1)
    i_r, i_s = shift_by(i_front + i_up, "x", 1), shift_by(i_back, "x", -1)
    t_r = shift_by(t_front, "z", 1)
    return i_own + i_r + i_s + i_y, t_own + t_r + t_s + t_y


def restore(grad, unit, length):
    along = jnp.sum(unit * grad, axis=-1, keepdims=True)
    return (grad - unit * along) / length


def per_device(photo, text, matching_index, warmth, shift):
    n = photo.shape[0]
    yl, x, yh, z, c = (lax.axis_index(a) for a in AXES)
    nx, nz = lax.axis_size("x"), lax.axis_size("z")
    ncol = lax.axis_size("yh") * nz * 2
    photo_scaled, photo_unit, photo_len, text_unit, text_len = normalize(warmth, photo, text)

    col = (yh * nz + z) * 2 + c
    row = yl * nx + x
    places = [(yl ^ dy) * nx + (x + dx) % nx for dx, dy in PLACES]
    match = jnp.concatenate([lax.dynamic_slice(matching_index, ((r * ncol + col) * n,), (n,)) for r in places])
    mine, other = ([((yh ^ dy) * nz + (z + dz) % nz) * 2 + (c ^ k) for dz, dy in PLACES] for k in (0, 1))
    cols = mine[:4] + other[:4] + mine[4:] + other[4:]
    bases = jnp.stack([(row * ncol + q) * n for q in cols]).astype(jnp.int32)

    hold = lax.optimization_barrier
    (near_i, near), far_i, far, (match, bases) = gather_shares(photo_scaled, text_unit, (match[:, None], bases))
    near = jnp.concatenate(near)
    near = (near, shift_by(near, "c", 1))
    parts = [((k, 4 * n),) for k in (0, 1)]
    gi_near, gt_a = pair_gradients(shift, near_i, match[: 4 * n], near, parts, bases[:8])
    gi_near, far_i, far = hold((gi_near, far_i, far))
    last = shift_by(far[1], "z", -1)
    gi_far, gt_b = pair_gradients(shift, far_i, match[4 * n :], near, parts, bases[:8])
    gi_far, last = hold((gi_far, last))
    far = jnp.concatenate([far[0], last, *far[1:]])
    far = (far, shift_by(far, "c", 1))
    gi, gt_far = pair_gradients(shift, near_i + far_i, match, far, parts, bases[8:], sums=gi_near + gi_far)
    gt_near = [a + b for a, b in zip(gt_a, gt_b)]
    photo_grad, text_grad = reduce_shares(gi, gt_near, gt_far)
    photo_grad = photo_grad * jnp.exp(warmth)
    return restore(photo_grad, photo_unit, photo_len), restore(text_grad, text_unit, text_len)


def solution(mesh):
    fine = Mesh(mesh.devices.reshape(2, 4, 2, 4, 2), AXES)
    spec = P(AXES, None)
    return jax.shard_map(
        per_device,
        mesh=fine,
        in_specs=(spec, spec, P(), P(), P()),
        out_specs=(spec, spec),
        check_vma=False,
    )
```

```python
import functools

import jax
import jax.numpy as jnp
from jax import lax
from jax.experimental import pallas as pl
from jax.experimental.pallas import tpu as pltpu
from jax.sharding import Mesh
from jax.sharding import PartitionSpec as P

EPS = 1e-06
F32 = jnp.float32
BF16 = jnp.bfloat16
F8 = jnp.float8_e4m3fn
P_HI, P_LO = 2.0**8, 2.0**17
TXT_HI, TXT_LO = 2.0**8, 2.0**17
IMG_HI, IMG_LO = 2.0**1, 2.0**10
AXES = ("yl", "x", "yh", "z", "c")
PLACES = ((0, 0), (-1, 0), (1, 0), (0, 1), (2, 0), (1, 1), (-1, 1), (2, 1))


def shift_by(value, axis, steps):
    count = lax.axis_size(axis)
    return lax.ppermute(value, axis, [(i, (i + steps) % count) for i in range(count)])


def mm(a, b, ca, cb):
    return lax.dot_general(a, b, (((ca,), (cb,)), ((), ())), preferred_element_type=F32)


def halves(x):
    hi = x.astype(BF16)
    return hi, (x - hi.astype(F32)).astype(BF16)


def eighths(hi, lo, hi_scale, lo_scale):
    return (hi.astype(F32) * hi_scale).astype(F8), (lo.astype(F32) * lo_scale).astype(F8)


def normalize_kernel(warmth, photo, text, photo_scaled, photo_unit, photo_len, text_unit, text_len):
    for raw, unit, length in ((photo, photo_unit, photo_len), (text, text_unit, text_len)):
        x = raw[...]
        size = jnp.sqrt(jnp.sum(x * x, axis=-1, keepdims=True) + EPS)
        unit[...] = x / size
        length[...] = size
    photo_scaled[...] = photo_unit[...] * jnp.exp(warmth[...])


def normalize(warmth, photo, text):
    n, d = photo.shape
    vm = pl.BlockSpec(memory_space=pltpu.VMEM)
    full = jax.ShapeDtypeStruct((n, d), F32)
    one = jax.ShapeDtypeStruct((n, 1), F32)
    return pl.pallas_call(
        normalize_kernel,
        in_specs=[vm, vm, vm],
        out_specs=[vm] * 5,
        out_shape=[full, full, one, full, one],
    )(warmth.reshape(1, 1), photo, text)


def pairs_kernel(bases, shift, match, *refs, shares, parts, n, ti, tj, more):
    imgs, refs = refs[:shares], refs[shares:]
    gi_in, refs = refs[: shares * more], refs[shares * more :]
    count = sum(len(p) for p in parts)
    txts, gi_out, refs = refs[:count], refs[count : count + shares], refs[count + shares :]
    gt_out = refs[: len(parts)]
    gi, gt, raw, ah, al, bh, bl, ah8, al8, bh8, bl8, img_in, img_out, sum_in, txt_in, txt_out = refs[len(parts) :]
    j = pl.program_id(0)
    last = len(parts) - 1

    def text_in(k):
        row, copies = 0, []
        for i, q in enumerate(parts[k]):
            copies.append(pltpu.make_async_copy(txts[q[0]], raw.at[k % 2, pl.ds(row, q[1])], txt_in.at[k % 2, i]))
            row += q[1]
        return copies

    def text_out(k):
        return [pltpu.make_async_copy(gt.at[k % 2], gt_out[k], txt_out.at[k % 2])]

    @pl.when(j == 0)
    def _():
        per = tj // n
        copies = [
            pltpu.make_async_copy(imgs[k], gt.at[k // per, pl.ds(k % per * n, n)], img_in.at[k]) for k in range(shares)
        ]
        sums = [pltpu.make_async_copy(gi_in[k], gi.at[pl.ds(k * n, n)], sum_in.at[k]) for k in range(shares * more)]
        for c in copies + text_in(0) + sums:
            c.start()
        for k, c in enumerate(copies):
            c.wait()
            rows = pl.ds(k * n, n)
            hi, lo = halves(gt[k // per, pl.ds(k % per * n, n), :])
            ah[rows, :], al[rows, :] = hi, lo
            ah8[rows, :], al8[rows, :] = eighths(hi, lo, IMG_HI, IMG_LO)
        for c in sums:
            c.wait()
        if not more:
            gi[...] = jnp.zeros_like(gi)

    for k in range(last + 1):

        @pl.when(j == k)
        def _():
            if k < last:
                for c in text_in(k + 1):
                    c.start()
            for c in text_in(k):
                c.wait()
            if k >= 2:
                for c in text_out(k - 2):
                    c.wait()

    slot = j % 2
    hi, lo = halves(raw[slot])
    bh[...], bl[...] = hi, lo
    bh8[...], bl8[...] = eighths(hi, lo, TXT_HI, TXT_LO)
    gt[slot] = jnp.zeros((tj, gt.shape[2]), F32)
    lane = lax.broadcasted_iota(jnp.int32, (1, n), 1)
    per = tj // n
    col = jnp.concatenate([lane + bases[j * per + q] for q in range(per)], axis=1)

    def step(i, c):
        rows = pl.ds(pl.multiple_of(i * ti, ti), ti)
        a_h = ah[rows, :]
        a_l = al[rows, :]
        b_h = bh[...]
        b_l = bl[...]
        s = mm(a_h, b_h, 1, 1) + mm(a_h, b_l, 1, 1) + mm(a_l, b_h, 1, 1)
        p = 1.0 / (1.0 + jnp.exp(-(s + shift[0])))
        p = jnp.where(match[rows, :] == col, p - 1.0, p)
        p_h, p_l = halves(p)
        p_h8, p_l8 = eighths(p_h, p_l, P_HI, P_LO)
        cross = mm(p_h8, bl8[...], 1, 0) + mm(p_l8, bh8[...], 1, 0)
        gi[rows, :] += mm(p_h, b_h, 1, 0) + cross * (1.0 / (P_HI * TXT_LO))
        cross = mm(p_h8, al8[rows, :], 0, 0) + mm(p_l8, ah8[rows, :], 0, 0)
        gt[slot] += mm(p_h, a_h, 0, 0) + cross * (1.0 / (P_HI * IMG_LO))
        return c

    lax.fori_loop(0, shares * n // ti, step, 0)

    for k in range(last + 1):

        @pl.when(j == k)
        def _():
            for c in text_out(k):
                c.start()

    @pl.when(j == last)
    def _():
        copies = [pltpu.make_async_copy(gi.at[pl.ds(k * n, n)], gi_out[k], img_out.at[k]) for k in range(shares)]
        for c in copies:
            c.start()
        for c in copies + text_out(last - 1) + text_out(last):
            c.wait()


def pair_gradients(shift, imgs, match, txts, parts, bases, sums=()):
    n, d = imgs[0].shape
    rows, tj = len(imgs) * n, sum(q[1] for q in parts[0])
    cols = len(parts) * tj
    sm, vm, far = (pl.BlockSpec(memory_space=m) for m in (pltpu.SMEM, pltpu.VMEM, pl.ANY))
    out = [jax.ShapeDtypeStruct((size, d), F32) for size in [n] * len(imgs) + [tj] * len(parts)]
    out = pl.pallas_call(
        functools.partial(pairs_kernel, shares=len(imgs), parts=parts, n=n, ti=rows, tj=tj, more=int(len(sums) > 0)),
        grid=(len(parts),),
        in_specs=[sm, sm, vm] + [far] * (len(imgs) + len(sums) + len(txts)),
        out_specs=[far] * len(out),
        scratch_shapes=[pltpu.VMEM((rows, d), F32)]
        + [pltpu.VMEM((2, tj, d), F32)] * 2
        + [pltpu.VMEM((rows, d), BF16)] * 2
        + [pltpu.VMEM((tj, d), BF16)] * 2
        + [pltpu.VMEM((rows, d), F8)] * 2
        + [pltpu.VMEM((tj, d), F8)] * 2
        + [pltpu.SemaphoreType.DMA((len(imgs),))] * 3
        + [pltpu.SemaphoreType.DMA((2, 4)), pltpu.SemaphoreType.DMA((2,))],
        out_shape=out,
        compiler_params=pltpu.CompilerParams(vmem_limit_bytes=58 * 2**20),
        cost_estimate=pl.CostEstimate(
            flops=18 * rows * cols * d, bytes_accessed=8 * (rows + cols) * d, transcendentals=2 * rows * cols
        ),
    )(bases, shift, match, *imgs, *sums, *txts)
    return out[: len(imgs)], out[len(imgs) :]


def gather_shares(photo, text, index):
    hold = lax.optimization_barrier
    i_back, i_front = shift_by(photo, "x", 1), shift_by(photo, "x", -1)
    t_back, t_front = shift_by(text, "z", 1), shift_by(text, "z", -1)
    i_twin = shift_by(photo, "yl", 1)
    i_back, i_front, t_back, t_front, i_twin, text, index = hold((i_back, i_front, t_back, t_front, i_twin, text, index))
    t_twin = shift_by(text, "yh", 1)
    i_far = shift_by(i_back, "x", 1)
    i_twin_front = shift_by(i_twin, "x", -1)
    other = [shift_by(share, "c", 1) for share in (text, t_back)]
    t_twin, i_far, i_twin_front, i_twin, other = hold((t_twin, i_far, i_twin_front, i_twin, other))
    t_twin_front, t_twin_back = shift_by(t_twin, "z", -1), shift_by(t_twin, "z", 1)
    i_twin_far, i_twin_back = shift_by(i_twin_front, "x", -1), shift_by(i_twin, "x", 1)
    near = [photo, i_back, i_front, i_twin], [text, t_back, t_front, t_twin]
    near[1].extend(other + [shift_by(share, "c", 1) for share in (t_front, t_twin)])
    return near, [i_far, i_twin_front, i_twin_back, i_twin_far], [t_back, t_twin_front, t_twin_back], index


def split_rows(x, n):
    return [x[k : k + n] for k in range(0, x.shape[0], n)]


def reduce_shares(photo, text_near, text_far):
    hold = lax.optimization_barrier
    i_own, i_back, i_front, i_twin, i_far, i_twin_front, i_twin_back, i_twin_far = photo
    n = i_own.shape[0]
    i_up, i_down = shift_by(i_far, "x", 1), shift_by(i_twin_far, "x", -1)
    near, far = shift_by(text_near[1], "c", 1), text_far[1]
    near, far = hold((near, far))
    t_far, t_twin_front, t_twin_back, t_twin_far = split_rows(text_far[0] + shift_by(far, "c", 1), n)
    t_up, t_down = shift_by(t_far, "z", 1), shift_by(t_twin_far, "z", -1)
    t_own, t_back, t_front, t_twin = split_rows(text_near[0] + near, n)
    i_up, i_down, t_up, t_down, t_back = hold((i_up, i_down, t_up, t_down, t_back))
    i_p, i_q = shift_by(i_twin_front, "x", 1), shift_by(i_twin_back + i_down, "x", -1)
    t_p, t_q = shift_by(t_twin_front, "z", 1), shift_by(t_twin_back + t_down, "z", -1)
    t_s = shift_by(t_back, "z", -1)
    i_back, i_p, i_q = hold((i_back, i_p, i_q))
    i_y = shift_by(i_twin + i_p + i_q, "yl", 1)
    t_front, t_p, t_q = hold((t_front + t_up, t_p, t_q))
    t_y = shift_by(t_twin + t_p + t_q, "yh", 1)
    i_r, i_s = shift_by(i_front + i_up, "x", 1), shift_by(i_back, "x", -1)
    t_r = shift_by(t_front, "z", 1)
    return i_own + i_r + i_s + i_y, t_own + t_r + t_s + t_y


def restore(grad, unit, length):
    along = jnp.sum(unit * grad, axis=-1, keepdims=True)
    return (grad - unit * along) / length


def per_device(photo, text, matching_index, warmth, shift):
    n = photo.shape[0]
    yl, x, yh, z, c = (lax.axis_index(a) for a in AXES)
    nx, nz = lax.axis_size("x"), lax.axis_size("z")
    ncol = lax.axis_size("yh") * nz * 2
    photo_scaled, photo_unit, photo_len, text_unit, text_len = normalize(warmth, photo, text)

    col = (yh * nz + z) * 2 + c
    row = yl * nx + x
    places = [(yl ^ dy) * nx + (x + dx) % nx for dx, dy in PLACES]
    match = jnp.concatenate([lax.dynamic_slice(matching_index, ((r * ncol + col) * n,), (n,)) for r in places])
    mine, other = ([((yh ^ dy) * nz + (z + dz) % nz) * 2 + (c ^ k) for dz, dy in PLACES] for k in (0, 1))
    cols = mine[:4] + other[:4] + mine[4:] + other[4:]
    bases = jnp.stack([(row * ncol + q) * n for q in cols]).astype(jnp.int32)

    hold = lax.optimization_barrier
    (near_i, near), far_i, far, (match, bases) = gather_shares(photo_scaled, text_unit, (match[:, None], bases))
    parts = [[(k, n) for k in range(4)], [(k, n) for k in range(4, 8)]]
    gi_near, gt_a = pair_gradients(shift, near_i, match[: 4 * n], near, parts, bases[:8])
    gi_near, far_i, far = hold((gi_near, far_i, far))
    t_far, last = shift_by(far[0], "z", 1), shift_by(far[1], "z", -1)
    gi_far, gt_b = pair_gradients(shift, far_i, match[4 * n :], near, parts, bases[:8])
    other = [shift_by(share, "c", 1) for share in far[1:]]
    gi_far, last, t_far, other = hold((gi_far, last, t_far, other))
    far = [t_far, *far[1:], last, shift_by(t_far, "c", 1), *other, shift_by(last, "c", 1)]
    gi, gt_far = pair_gradients(shift, near_i + far_i, match, far, parts, bases[8:], sums=gi_near + gi_far)
    gt_near = [a + b for a, b in zip(gt_a, gt_b)]
    photo_grad, text_grad = reduce_shares(gi, gt_near, gt_far)
    photo_grad = photo_grad * jnp.exp(warmth)
    return restore(photo_grad, photo_unit, photo_len), restore(text_grad, text_unit, text_len)


def solution(mesh):
    fine = Mesh(mesh.devices.reshape(2, 4, 2, 4, 2), AXES)
    spec = P(AXES, None)
    return jax.shard_map(
        per_device,
        mesh=fine,
        in_specs=(spec, spec, P(), P(), P()),
        out_specs=(spec, spec),
        check_vma=False,
    )
```

```python
import functools

import jax
import jax.numpy as jnp
from jax import lax
from jax.experimental import pallas as pl
from jax.experimental.pallas import tpu as pltpu
from jax.sharding import Mesh
from jax.sharding import PartitionSpec as P

EPS = 1e-06
F32 = jnp.float32
BF16 = jnp.bfloat16
F8 = jnp.float8_e4m3fn
P_HI, P_LO = 2.0**8, 2.0**17
TXT_HI, TXT_LO = 2.0**8, 2.0**17
IMG_HI, IMG_LO = 2.0**1, 2.0**10
AXES = ("yl", "x", "yh", "z", "c")
PLACES = ((0, 0), (-1, 0), (1, 0), (0, 1), (2, 0), (1, 1), (-1, 1), (2, 1))


def shift_by(value, axis, steps):
    count = lax.axis_size(axis)
    return lax.ppermute(value, axis, [(i, (i + steps) % count) for i in range(count)])


def mm(a, b, ca, cb):
    return lax.dot_general(a, b, (((ca,), (cb,)), ((), ())), preferred_element_type=F32)


def halves(x):
    hi = x.astype(BF16)
    return hi, (x - hi.astype(F32)).astype(BF16)


def eighths(hi, lo, hi_scale, lo_scale):
    return (hi.astype(F32) * hi_scale).astype(F8), (lo.astype(F32) * lo_scale).astype(F8)


def normalize_kernel(warmth, photo, text, photo_scaled, photo_unit, photo_len, text_unit, text_len):
    for raw, unit, length in ((photo, photo_unit, photo_len), (text, text_unit, text_len)):
        x = raw[...]
        size = jnp.sqrt(jnp.sum(x * x, axis=-1, keepdims=True) + EPS)
        unit[...] = x / size
        length[...] = size
    photo_scaled[...] = photo_unit[...] * jnp.exp(warmth[...])


def normalize(warmth, photo, text):
    n, d = photo.shape
    vm = pl.BlockSpec(memory_space=pltpu.VMEM)
    full = jax.ShapeDtypeStruct((n, d), F32)
    one = jax.ShapeDtypeStruct((n, 1), F32)
    return pl.pallas_call(
        normalize_kernel,
        in_specs=[vm, vm, vm],
        out_specs=[vm] * 5,
        out_shape=[full, full, one, full, one],
    )(warmth.reshape(1, 1), photo, text)


def pairs_kernel(bases, shift, match, *refs, shares, parts, n, ti, tj, more):
    imgs, refs = refs[:shares], refs[shares:]
    gi_in, refs = refs[: shares * more], refs[shares * more :]
    count = sum(len(p) for p in parts)
    txts, gi_out, refs = refs[:count], refs[count : count + shares], refs[count + shares :]
    gt_out = refs[: len(parts)]
    gi, gt, raw, ah, al, bh, bl, ah8, al8, bh8, bl8, img_in, img_out, sum_in, txt_in, txt_out = refs[len(parts) :]
    j = pl.program_id(0)
    last = len(parts) - 1

    def text_in(k):
        row, copies = 0, []
        for i, q in enumerate(parts[k]):
            copies.append(pltpu.make_async_copy(txts[q[0]], raw.at[k % 2, pl.ds(row, q[1])], txt_in.at[k % 2, i]))
            row += q[1]
        return copies

    def text_out(k):
        return [pltpu.make_async_copy(gt.at[k % 2], gt_out[k], txt_out.at[k % 2])]

    @pl.when(j == 0)
    def _():
        per = tj // n
        copies = [
            pltpu.make_async_copy(imgs[k], gt.at[k // per, pl.ds(k % per * n, n)], img_in.at[k]) for k in range(shares)
        ]
        sums = [pltpu.make_async_copy(gi_in[k], gi.at[pl.ds(k * n, n)], sum_in.at[k]) for k in range(shares * more)]
        for c in copies + text_in(0) + sums:
            c.start()
        for k, c in enumerate(copies):
            c.wait()
            rows = pl.ds(k * n, n)
            hi, lo = halves(gt[k // per, pl.ds(k % per * n, n), :])
            ah[rows, :], al[rows, :] = hi, lo
            ah8[rows, :], al8[rows, :] = eighths(hi, lo, IMG_HI, IMG_LO)
        for c in sums:
            c.wait()
        if not more:
            gi[...] = jnp.zeros_like(gi)

    for k in range(last + 1):

        @pl.when(j == k)
        def _():
            if k < last:
                for c in text_in(k + 1):
                    c.start()
            for c in text_in(k):
                c.wait()
            if k >= 2:
                for c in text_out(k - 2):
                    c.wait()

    slot = j % 2
    hi, lo = halves(raw[slot])
    bh[...], bl[...] = hi, lo
    bh8[...], bl8[...] = eighths(hi, lo, TXT_HI, TXT_LO)
    gt[slot] = jnp.zeros((tj, gt.shape[2]), F32)
    lane = lax.broadcasted_iota(jnp.int32, (1, n), 1)
    per = tj // n
    col = jnp.concatenate([lane + bases[j * per + q] for q in range(per)], axis=1)

    def step(i, c):
        rows = pl.ds(pl.multiple_of(i * ti, ti), ti)
        a_h = ah[rows, :]
        a_l = al[rows, :]
        b_h = bh[...]
        b_l = bl[...]
        s = mm(a_h, b_h, 1, 1) + mm(a_h, b_l, 1, 1) + mm(a_l, b_h, 1, 1)
        p = 1.0 / (1.0 + jnp.exp(-(s + shift[0])))
        p = jnp.where(match[rows, :] == col, p - 1.0, p)
        p_h, p_l = halves(p)
        p_h8, p_l8 = eighths(p_h, p_l, P_HI, P_LO)
        cross = mm(p_h8, bl8[...], 1, 0) + mm(p_l8, bh8[...], 1, 0)
        gi[rows, :] += mm(p_h, b_h, 1, 0) + cross * (1.0 / (P_HI * TXT_LO))
        cross = mm(p_h8, al8[rows, :], 0, 0) + mm(p_l8, ah8[rows, :], 0, 0)
        gt[slot] += mm(p_h, a_h, 0, 0) + cross * (1.0 / (P_HI * IMG_LO))
        return c

    lax.fori_loop(0, shares * n // ti, step, 0)

    for k in range(last + 1):

        @pl.when(j == k)
        def _():
            for c in text_out(k):
                c.start()

    @pl.when(j == last)
    def _():
        copies = [pltpu.make_async_copy(gi.at[pl.ds(k * n, n)], gi_out[k], img_out.at[k]) for k in range(shares)]
        for c in copies:
            c.start()
        for c in copies + text_out(last - 1) + text_out(last):
            c.wait()


def pair_gradients(shift, imgs, match, txts, parts, bases, sums=()):
    n, d = imgs[0].shape
    rows, tj = len(imgs) * n, sum(q[1] for q in parts[0])
    cols = len(parts) * tj
    sm, vm, far = (pl.BlockSpec(memory_space=m) for m in (pltpu.SMEM, pltpu.VMEM, pl.ANY))
    out = [jax.ShapeDtypeStruct((size, d), F32) for size in [n] * len(imgs) + [tj] * len(parts)]
    out = pl.pallas_call(
        functools.partial(pairs_kernel, shares=len(imgs), parts=parts, n=n, ti=rows, tj=tj, more=int(len(sums) > 0)),
        grid=(len(parts),),
        in_specs=[sm, sm, vm] + [far] * (len(imgs) + len(sums) + len(txts)),
        out_specs=[far] * len(out),
        scratch_shapes=[pltpu.VMEM((rows, d), F32)]
        + [pltpu.VMEM((2, tj, d), F32)] * 2
        + [pltpu.VMEM((rows, d), BF16)] * 2
        + [pltpu.VMEM((tj, d), BF16)] * 2
        + [pltpu.VMEM((rows, d), F8)] * 2
        + [pltpu.VMEM((tj, d), F8)] * 2
        + [pltpu.SemaphoreType.DMA((len(imgs),))] * 3
        + [pltpu.SemaphoreType.DMA((2, 4)), pltpu.SemaphoreType.DMA((2,))],
        out_shape=out,
        compiler_params=pltpu.CompilerParams(vmem_limit_bytes=58 * 2**20),
        cost_estimate=pl.CostEstimate(
            flops=18 * rows * cols * d, bytes_accessed=8 * (rows + cols) * d, transcendentals=2 * rows * cols
        ),
    )(bases, shift, match, *imgs, *sums, *txts)
    return out[: len(imgs)], out[len(imgs) :]


def gather_shares(photo, text, index):
    hold = lax.optimization_barrier
    i_back, i_front = shift_by(photo, "x", 1), shift_by(photo, "x", -1)
    t_back, t_front = shift_by(text, "z", 1), shift_by(text, "z", -1)
    i_twin = shift_by(photo, "yl", 1)
    i_back, i_front, i_twin, text, index = hold((i_back, i_front, i_twin, text, index))
    t_twin = shift_by(text, "yh", 1)
    i_far = shift_by(i_back, "x", 1)
    i_twin_front = shift_by(i_twin, "x", -1)
    t_twin, t_back, t_front, i_far, i_twin_front, i_twin = hold((t_twin, t_back, t_front, i_far, i_twin_front, i_twin))
    t_twin_front, t_twin_back = shift_by(t_twin, "z", -1), shift_by(t_twin, "z", 1)
    i_twin_far, i_twin_back = shift_by(i_twin_front, "x", -1), shift_by(i_twin, "x", 1)
    near = [photo, i_back, i_front, i_twin], [text, t_back, t_front, t_twin]
    near[1].extend([shift_by(share, "c", 1) for share in near[1]])
    return near, [i_far, i_twin_front, i_twin_back, i_twin_far], [t_back, t_twin_front, t_twin_back], index


def split_rows(x, n):
    return [x[k : k + n] for k in range(0, x.shape[0], n)]


def reduce_shares(photo, text_near, text_far):
    hold = lax.optimization_barrier
    i_own, i_back, i_front, i_twin, i_far, i_twin_front, i_twin_back, i_twin_far = photo
    n = i_own.shape[0]
    i_up, i_down = shift_by(i_far, "x", 1), shift_by(i_twin_far, "x", -1)
    near, far = shift_by(text_near[1], "c", 1), text_far[1]
    near, far = hold((near, far))
    t_far, t_twin_front, t_twin_back, t_twin_far = split_rows(text_far[0] + shift_by(far, "c", 1), n)
    t_up, t_down = shift_by(t_far, "z", 1), shift_by(t_twin_far, "z", -1)
    t_own, t_back, t_front, t_twin = split_rows(text_near[0] + near, n)
    i_up, i_down, t_up, t_down, t_back = hold((i_up, i_down, t_up, t_down, t_back))
    i_p, i_q = shift_by(i_twin_front, "x", 1), shift_by(i_twin_back + i_down, "x", -1)
    t_p, t_q = shift_by(t_twin_front, "z", 1), shift_by(t_twin_back + t_down, "z", -1)
    t_s = shift_by(t_back, "z", -1)
    i_back, i_p, i_q = hold((i_back, i_p, i_q))
    i_y = shift_by(i_twin + i_p + i_q, "yl", 1)
    t_front, t_p, t_q = hold((t_front + t_up, t_p, t_q))
    t_y = shift_by(t_twin + t_p + t_q, "yh", 1)
    i_r, i_s = shift_by(i_front + i_up, "x", 1), shift_by(i_back, "x", -1)
    t_r = shift_by(t_front, "z", 1)
    return i_own + i_r + i_s + i_y, t_own + t_r + t_s + t_y


def restore(grad, unit, length):
    along = jnp.sum(unit * grad, axis=-1, keepdims=True)
    return (grad - unit * along) / length


def per_device(photo, text, matching_index, warmth, shift):
    n = photo.shape[0]
    yl, x, yh, z, c = (lax.axis_index(a) for a in AXES)
    nx, nz = lax.axis_size("x"), lax.axis_size("z")
    ncol = lax.axis_size("yh") * nz * 2
    photo_scaled, photo_unit, photo_len, text_unit, text_len = normalize(warmth, photo, text)

    col = (yh * nz + z) * 2 + c
    row = yl * nx + x
    places = [(yl ^ dy) * nx + (x + dx) % nx for dx, dy in PLACES]
    match = jnp.concatenate([lax.dynamic_slice(matching_index, ((r * ncol + col) * n,), (n,)) for r in places])
    mine, other = ([((yh ^ dy) * nz + (z + dz) % nz) * 2 + (c ^ k) for dz, dy in PLACES] for k in (0, 1))
    cols = mine[:4] + other[:4] + mine[4:] + other[4:]
    bases = jnp.stack([(row * ncol + q) * n for q in cols]).astype(jnp.int32)

    hold = lax.optimization_barrier
    (near_i, near), far_i, far, (match, bases) = gather_shares(photo_scaled, text_unit, (match[:, None], bases))
    parts = [[(k, n) for k in range(4)], [(k, n) for k in range(4, 8)]]
    gi_near, gt_a = pair_gradients(shift, near_i, match[: 4 * n], near, parts, bases[:8])
    gi_near, far_i, far = hold((gi_near, far_i, far))
    t_far, last = shift_by(far[0], "z", 1), shift_by(far[1], "z", -1)
    gi_far, gt_b = pair_gradients(shift, far_i, match[4 * n :], near, parts, bases[:8])
    other = [shift_by(share, "c", 1) for share in far[1:]]
    gi_far, last, t_far, other = hold((gi_far, last, t_far, other))
    far = [t_far, *far[1:], last, shift_by(t_far, "c", 1), *other, shift_by(last, "c", 1)]
    gi, gt_far = pair_gradients(shift, near_i + far_i, match, far, parts, bases[8:], sums=gi_near + gi_far)
    gt_near = [a + b for a, b in zip(gt_a, gt_b)]
    photo_grad, text_grad = reduce_shares(gi, gt_near, gt_far)
    photo_grad = photo_grad * jnp.exp(warmth)
    return restore(photo_grad, photo_unit, photo_len), restore(text_grad, text_unit, text_len)


def solution(mesh):
    fine = Mesh(mesh.devices.reshape(2, 4, 2, 4, 2), AXES)
    spec = P(AXES, None)
    return jax.shard_map(
        per_device,
        mesh=fine,
        in_specs=(spec, spec, P(), P(), P()),
        out_specs=(spec, spec),
        check_vma=False,
    )
```

```python
import functools

import jax
import jax.numpy as jnp
from jax import lax
from jax.experimental import pallas as pl
from jax.experimental.pallas import tpu as pltpu
from jax.sharding import Mesh
from jax.sharding import PartitionSpec as P

EPS = 1e-06
F32 = jnp.float32
BF16 = jnp.bfloat16
F8 = jnp.float8_e4m3fn
P_HI, P_LO = 2.0**8, 2.0**17
TXT_HI, TXT_LO = 2.0**8, 2.0**17
IMG_HI, IMG_LO = 2.0**1, 2.0**10
AXES = ("yl", "x", "yh", "z", "c")
PLACES = ((0, 0), (-1, 0), (1, 0), (0, 1), (2, 0), (1, 1), (-1, 1), (2, 1))


def shift_by(value, axis, steps):
    count = lax.axis_size(axis)
    return lax.ppermute(value, axis, [(i, (i + steps) % count) for i in range(count)])


def mm(a, b, ca, cb):
    return lax.dot_general(a, b, (((ca,), (cb,)), ((), ())), preferred_element_type=F32)


def halves(x):
    hi = x.astype(BF16)
    return hi, (x - hi.astype(F32)).astype(BF16)


def eighths(hi, lo, hi_scale, lo_scale):
    return (hi.astype(F32) * hi_scale).astype(F8), (lo.astype(F32) * lo_scale).astype(F8)


def normalize_kernel(warmth, photo, text, photo_scaled, photo_unit, photo_len, text_unit, text_len):
    for raw, unit, length in ((photo, photo_unit, photo_len), (text, text_unit, text_len)):
        x = raw[...]
        size = jnp.sqrt(jnp.sum(x * x, axis=-1, keepdims=True) + EPS)
        unit[...] = x / size
        length[...] = size
    photo_scaled[...] = photo_unit[...] * jnp.exp(warmth[...])


def normalize(warmth, photo, text):
    n, d = photo.shape
    vm = pl.BlockSpec(memory_space=pltpu.VMEM)
    full = jax.ShapeDtypeStruct((n, d), F32)
    one = jax.ShapeDtypeStruct((n, 1), F32)
    return pl.pallas_call(
        normalize_kernel,
        in_specs=[vm, vm, vm],
        out_specs=[vm] * 5,
        out_shape=[full, full, one, full, one],
    )(warmth.reshape(1, 1), photo, text)


def pairs_kernel(bases, shift, match, *refs, shares, parts, n, ti, tj, more):
    imgs, refs = refs[:shares], refs[shares:]
    gi_in, refs = refs[: shares * more], refs[shares * more :]
    count = sum(len(p) for p in parts)
    txts, gi_out, refs = refs[:count], refs[count : count + shares], refs[count + shares :]
    gt_out = refs[: len(parts)]
    gi, gt, raw, ah, al, bh, bl, ah8, al8, bh8, bl8, img_in, img_out, sum_in, txt_in, txt_out = refs[len(parts) :]
    j = pl.program_id(0)
    last = len(parts) - 1

    def text_in(k):
        row, copies = 0, []
        for i, q in enumerate(parts[k]):
            copies.append(pltpu.make_async_copy(txts[q[0]], raw.at[k % 2, pl.ds(row, q[1])], txt_in.at[k % 2, i]))
            row += q[1]
        return copies

    def text_out(k):
        return [pltpu.make_async_copy(gt.at[k % 2], gt_out[k], txt_out.at[k % 2])]

    @pl.when(j == 0)
    def _():
        per = tj // n
        copies = [
            pltpu.make_async_copy(imgs[k], gt.at[k // per, pl.ds(k % per * n, n)], img_in.at[k]) for k in range(shares)
        ]
        sums = [pltpu.make_async_copy(gi_in[k], gi.at[pl.ds(k * n, n)], sum_in.at[k]) for k in range(shares * more)]
        for c in copies + text_in(0) + sums:
            c.start()
        for k, c in enumerate(copies):
            c.wait()
            rows = pl.ds(k * n, n)
            hi, lo = halves(gt[k // per, pl.ds(k % per * n, n), :])
            ah[rows, :], al[rows, :] = hi, lo
            ah8[rows, :], al8[rows, :] = eighths(hi, lo, IMG_HI, IMG_LO)
        for c in sums:
            c.wait()
        if not more:
            gi[...] = jnp.zeros_like(gi)

    for k in range(last + 1):

        @pl.when(j == k)
        def _():
            if k < last:
                for c in text_in(k + 1):
                    c.start()
            for c in text_in(k):
                c.wait()
            if k >= 2:
                for c in text_out(k - 2):
                    c.wait()

    slot = j % 2
    hi, lo = halves(raw[slot])
    bh[...], bl[...] = hi, lo
    bh8[...], bl8[...] = eighths(hi, lo, TXT_HI, TXT_LO)
    gt[slot] = jnp.zeros((tj, gt.shape[2]), F32)
    lane = lax.broadcasted_iota(jnp.int32, (1, n), 1)
    per = tj // n
    col = jnp.concatenate([lane + bases[j * per + q] for q in range(per)], axis=1)

    def step(i, c):
        rows = pl.ds(pl.multiple_of(i * ti, ti), ti)
        a_h = ah[rows, :]
        a_l = al[rows, :]
        b_h = bh[...]
        b_l = bl[...]
        s = mm(a_h, b_h, 1, 1) + mm(a_h, b_l, 1, 1) + mm(a_l, b_h, 1, 1)
        p = 1.0 / (1.0 + jnp.exp(-(s + shift[0])))
        p = jnp.where(match[rows, :] == col, p - 1.0, p)
        p_h, p_l = halves(p)
        p_h8, p_l8 = eighths(p_h, p_l, P_HI, P_LO)
        cross = mm(p_h8, bl8[...], 1, 0) + mm(p_l8, bh8[...], 1, 0)
        gi[rows, :] += mm(p_h, b_h, 1, 0) + cross * (1.0 / (P_HI * TXT_LO))
        cross = mm(p_h8, al8[rows, :], 0, 0) + mm(p_l8, ah8[rows, :], 0, 0)
        gt[slot] += mm(p_h, a_h, 0, 0) + cross * (1.0 / (P_HI * IMG_LO))
        return c

    lax.fori_loop(0, shares * n // ti, step, 0)

    for k in range(last + 1):

        @pl.when(j == k)
        def _():
            for c in text_out(k):
                c.start()

    @pl.when(j == last)
    def _():
        copies = [pltpu.make_async_copy(gi.at[pl.ds(k * n, n)], gi_out[k], img_out.at[k]) for k in range(shares)]
        for c in copies:
            c.start()
        for c in copies + text_out(last - 1) + text_out(last):
            c.wait()


def pair_gradients(shift, imgs, match, txts, parts, bases, sums=()):
    n, d = imgs[0].shape
    rows, tj = len(imgs) * n, sum(q[1] for q in parts[0])
    cols = len(parts) * tj
    sm, vm, far = (pl.BlockSpec(memory_space=m) for m in (pltpu.SMEM, pltpu.VMEM, pl.ANY))
    out = [jax.ShapeDtypeStruct((size, d), F32) for size in [n] * len(imgs) + [tj] * len(parts)]
    out = pl.pallas_call(
        functools.partial(pairs_kernel, shares=len(imgs), parts=parts, n=n, ti=rows, tj=tj, more=int(len(sums) > 0)),
        grid=(len(parts),),
        in_specs=[sm, sm, vm] + [far] * (len(imgs) + len(sums) + len(txts)),
        out_specs=[far] * len(out),
        scratch_shapes=[pltpu.VMEM((rows, d), F32)]
        + [pltpu.VMEM((2, tj, d), F32)] * 2
        + [pltpu.VMEM((rows, d), BF16)] * 2
        + [pltpu.VMEM((tj, d), BF16)] * 2
        + [pltpu.VMEM((rows, d), F8)] * 2
        + [pltpu.VMEM((tj, d), F8)] * 2
        + [pltpu.SemaphoreType.DMA((len(imgs),))] * 3
        + [pltpu.SemaphoreType.DMA((2, 4)), pltpu.SemaphoreType.DMA((2,))],
        out_shape=out,
        compiler_params=pltpu.CompilerParams(vmem_limit_bytes=58 * 2**20),
        cost_estimate=pl.CostEstimate(
            flops=18 * rows * cols * d, bytes_accessed=8 * (rows + cols) * d, transcendentals=2 * rows * cols
        ),
    )(bases, shift, match, *imgs, *sums, *txts)
    return out[: len(imgs)], out[len(imgs) :]


def gather_shares(photo, text, index):
    hold = lax.optimization_barrier
    i_back, i_front = shift_by(photo, "x", 1), shift_by(photo, "x", -1)
    t_back, t_front = shift_by(text, "z", 1), shift_by(text, "z", -1)
    i_twin = shift_by(photo, "yl", 1)
    i_back, i_front, i_twin, text, index = hold((i_back, i_front, i_twin, text, index))
    t_twin = shift_by(text, "yh", 1)
    i_far = shift_by(i_back, "x", 1)
    i_twin_front = shift_by(i_twin, "x", -1)
    t_twin, t_back, t_front = hold((t_twin, t_back, t_front))
    i_far, i_twin_front, i_twin = hold((i_far, i_twin_front, i_twin))
    t_twin_front, t_twin_back = shift_by(t_twin, "z", -1), shift_by(t_twin, "z", 1)
    i_twin_far, i_twin_back = shift_by(i_twin_front, "x", -1), shift_by(i_twin, "x", 1)
    near = [photo, i_back, i_front, i_twin], [text, t_back, t_front, t_twin]
    near[1].extend([shift_by(share, "c", 1) for share in near[1]])
    return near, [i_far, i_twin_front, i_twin_back, i_twin_far], [t_back, t_twin_front, t_twin_back], index


def split_rows(x, n):
    return [x[k : k + n] for k in range(0, x.shape[0], n)]


def reduce_shares(photo, text_near, text_far):
    hold = lax.optimization_barrier
    i_own, i_back, i_front, i_twin, i_far, i_twin_front, i_twin_back, i_twin_far = photo
    n = i_own.shape[0]
    i_up, i_down = shift_by(i_far, "x", 1), shift_by(i_twin_far, "x", -1)
    near, far = shift_by(text_near[1], "c", 1), text_far[1]
    near, far = hold((near, far))
    t_far, t_twin_front, t_twin_back, t_twin_far = split_rows(text_far[0] + shift_by(far, "c", 1), n)
    t_up, t_down = shift_by(t_far, "z", 1), shift_by(t_twin_far, "z", -1)
    t_own, t_back, t_front, t_twin = split_rows(text_near[0] + near, n)
    i_up, i_down, t_up, t_down, t_back = hold((i_up, i_down, t_up, t_down, t_back))
    i_p, i_q = shift_by(i_twin_front, "x", 1), shift_by(i_twin_back + i_down, "x", -1)
    t_p, t_q = shift_by(t_twin_front, "z", 1), shift_by(t_twin_back + t_down, "z", -1)
    t_s = shift_by(t_back, "z", -1)
    i_back, i_p, i_q = hold((i_back, i_p, i_q))
    i_y = shift_by(i_twin + i_p + i_q, "yl", 1)
    t_front, t_p, t_q = hold((t_front + t_up, t_p, t_q))
    t_y = shift_by(t_twin + t_p + t_q, "yh", 1)
    i_r, i_s = shift_by(i_front + i_up, "x", 1), shift_by(i_back, "x", -1)
    t_r = shift_by(t_front, "z", 1)
    return i_own + i_r + i_s + i_y, t_own + t_r + t_s + t_y


def restore(grad, unit, length):
    along = jnp.sum(unit * grad, axis=-1, keepdims=True)
    return (grad - unit * along) / length


def per_device(photo, text, matching_index, warmth, shift):
    n = photo.shape[0]
    yl, x, yh, z, c = (lax.axis_index(a) for a in AXES)
    nx, nz = lax.axis_size("x"), lax.axis_size("z")
    ncol = lax.axis_size("yh") * nz * 2
    photo_scaled, photo_unit, photo_len, text_unit, text_len = normalize(warmth, photo, text)

    col = (yh * nz + z) * 2 + c
    row = yl * nx + x
    places = [(yl ^ dy) * nx + (x + dx) % nx for dx, dy in PLACES]
    match = jnp.concatenate([lax.dynamic_slice(matching_index, ((r * ncol + col) * n,), (n,)) for r in places])
    mine, other = ([((yh ^ dy) * nz + (z + dz) % nz) * 2 + (c ^ k) for dz, dy in PLACES] for k in (0, 1))
    cols = mine[:4] + other[:4] + mine[4:] + other[4:]
    bases = jnp.stack([(row * ncol + q) * n for q in cols]).astype(jnp.int32)

    hold = lax.optimization_barrier
    (near_i, near), far_i, far, (match, bases) = gather_shares(photo_scaled, text_unit, (match[:, None], bases))
    parts = [[(k, n) for k in range(4)], [(k, n) for k in range(4, 8)]]
    gi_near, gt_a = pair_gradients(shift, near_i, match[: 4 * n], near, parts, bases[:8])
    gi_near, far_i, far = hold((gi_near, far_i, far))
    t_far, last = shift_by(far[0], "z", 1), shift_by(far[1], "z", -1)
    gi_far, gt_b = pair_gradients(shift, far_i, match[4 * n :], near, parts, bases[:8])
    other = [shift_by(share, "c", 1) for share in far[1:]]
    gi_far, last, t_far, other = hold((gi_far, last, t_far, other))
    far = [t_far, *far[1:], last, shift_by(t_far, "c", 1), *other, shift_by(last, "c", 1)]
    gi, gt_far = pair_gradients(shift, near_i + far_i, match, far, parts, bases[8:], sums=gi_near + gi_far)
    gt_near = [a + b for a, b in zip(gt_a, gt_b)]
    photo_grad, text_grad = reduce_shares(gi, gt_near, gt_far)
    photo_grad = photo_grad * jnp.exp(warmth)
    return restore(photo_grad, photo_unit, photo_len), restore(text_grad, text_unit, text_len)


def solution(mesh):
    fine = Mesh(mesh.devices.reshape(2, 4, 2, 4, 2), AXES)
    spec = P(AXES, None)
    return jax.shard_map(
        per_device,
        mesh=fine,
        in_specs=(spec, spec, P(), P(), P()),
        out_specs=(spec, spec),
        check_vma=False,
    )
```
